256 devices in a mesh: var: 8 (over z), space: 32 (over x, y, core).
Axes of the slice: x: 4, y: 4, z: 8, core: 2. Of those that a mesh axis runs over, the one named last changes fastest.
Arguments:
- pixels: bfloat16 [96, 64, 4096], P('var', None, 'space'), may hold values from -6 to 6
- valid_mask: int32 [96], P('var'), may hold values from 0 to 1, as said below
- var_ids: int32 [96], P('var'), may hold values from 0 to 95, each once
- embed_weight: bfloat16 [96, 64, 1024], P('var'), may hold values from -0.75 to 0.75
- var_table: bfloat16 [96, 1024], replicated, may hold values from -3 to 3
- agg_query: float32 [1024], replicated, may hold values from -40 to 40
- agg_key: bfloat16 [1024, 1024], P('space'), may hold values from -0.1875 to 0.1875
- agg_value: bfloat16 [1024, 1024], replicated, may hold values from -0.1875 to 0.1875
- agg_out: bfloat16 [1024, 1024], replicated, may hold values from -0.1875 to 0.1875
- pos_embed: bfloat16 [4096, 1024], P('space'), may hold values from -3 to 3
- w_qkv: bfloat16 [1024, 3, 1024], P(None, None, 'var'), may hold values from -0.1875 to 0.1875
- w_out: bfloat16 [1024, 1024], P('var'), may hold values from -0.75 to 0.75
- w_up: bfloat16 [1024, 4096], P(None, 'var'), may hold values from -0.1875 to 0.1875
- w_down: bfloat16 [4096, 1024], P('var'), may hold values from -0.09375 to 0.09375
- cotangent: bfloat16 [4096, 1024], P('space'), may hold values from -6 to 6
Outputs:
- layer_out: bfloat16 [4096, 1024], P('space')
- grad_tokens: bfloat16 [4096, 1024], P('space')
- grad_qkv: float32 [1024, 3, 1024], P('space', None, 'var')
- grad_out: float32 [1024, 1024], P(('var', 'space'))
- grad_up: float32 [1024, 4096], P('space', 'var')
- grad_down: float32 [4096, 1024], P(('var', 'space'))
The draws below stay inside these ranges and needn't reach their ends.
Inputs may be any that keep to these rules, and one draw needn't show every extreme that they name: `valid_mask`: exactly 5 entries are 0, the others 1.
All inputs are finite; a program needn't handle non-finite values.
Results may differ from the reference program's by a relative error of at most 0.02.
The reference program's roundings to bfloat16 on the way count: a program that leaves them out, or rounds other values in their place, can miss the bound.
Values may be sent and summed in bfloat16 or wider, within the bound.
A program may use at most 128 MiB of HBM per device.

```python
import math
import jax
import jax.numpy as jnp
from jax import lax

V = 96
NDUMMY = 5
PIX = 64
D = 1024
H = 16
DH = 64
FF = 4096
PATCHES = 4096


def draw_valid_mask(key, part):
    key = jax.random.fold_in(key, 11)
    order = jax.random.permutation(key, V)
    return (order >= NDUMMY).astype(jnp.int32)


def draw_agg_query(key, part):
    key = jax.random.fold_in(key, 12)
    return jnp.clip(jax.random.normal(key, (D,), jnp.float32), -6.0, 6.0)


def draw_w_qkv(key, part):
    key = jax.random.fold_in(key, 13)
    base_key = jax.random.fold_in(key, 0)
    return jnp.clip(jax.random.normal(base_key, (D, 3, D), jnp.float32) * D ** (-0.5), -0.1875, 0.1875).astype(jnp.bfloat16)


def levels(own_key, extent, cuts, smallest, high):
    factor_of, own = 1.0, jax.random.fold_in(own_key, 6)
    for axis_at, blocks in cuts:
        heights = jnp.exp(jax.random.uniform(jax.random.fold_in(own, axis_at), (blocks,), jnp.float32, smallest / len(cuts), high / len(cuts)))
        factor_of = factor_of * jnp.repeat(heights, extent[axis_at] // blocks).reshape([-1 if axis == axis_at else 1 for axis in range(len(extent))])
    return factor_of


def scatter_about(key, dims, scale, reach, cuts=(), kind=jnp.bfloat16):
    level = levels(key, dims, cuts, -0.22, 0.18) if cuts else 1.0
    drawn = jax.random.normal(key, dims, jnp.float32) * scale * level
    return jnp.minimum(jnp.maximum(drawn, -reach), reach).astype(kind)


def setup_inputs(seed: int = 0) -> dict:
    keys = jax.random.split(jax.random.key(seed), 16)
    return {
        "pixels": scatter_about(keys[0], (V, PIX, PATCHES), 1.0, 6.0, ((0, 8), (2, 32))),
        "valid_mask": draw_valid_mask(jax.random.fold_in(keys[15], 71), 0),
        "var_ids": jax.random.permutation(keys[2], V).astype(jnp.int32),
        "embed_weight": scatter_about(keys[3], (V, PIX, D), PIX ** -0.5, 0.75, ((0, 8),)),
        "var_table": scatter_about(keys[4], (V, D), 0.5, 3.0),
        "agg_query": draw_agg_query(jax.random.fold_in(keys[15], 71), 0),
        "agg_key": scatter_about(keys[6], (D, D), D ** -0.5, 0.1875, ((0, 32),)),
        "agg_value": scatter_about(keys[7], (D, D), D ** -0.5, 0.1875),
        "agg_out": scatter_about(keys[8], (D, D), D ** -0.5, 0.1875),
        "pos_embed": scatter_about(keys[9], (PATCHES, D), 0.5, 3.0, ((0, 32),)),
        "w_qkv": draw_w_qkv(jax.random.fold_in(keys[15], 71), 0),
        "w_out": scatter_about(keys[11], (D, D), (D // 16) ** -0.5, 0.75, ((0, 8),)),
        "w_up": scatter_about(keys[12], (D, FF), D ** -0.5, 0.1875, ((1, 8),)),
        "w_down": scatter_about(keys[13], (FF, D), FF ** -0.5, 0.09375, ((0, 8),)),
        "cotangent": scatter_about(keys[14], (PATCHES, D), 1.0, 6.0, ((0, 32),)),
    }


EPSILON = 1e-05
MASK_FLOOR = -1e+30
HIGHEST = lax.Precision.HIGHEST

def matmul(left, right):
    return jnp.dot(left, right, preferred_element_type=jnp.float32)

def layer_norm(inputs):
    values = inputs.astype(jnp.float32)
    centred = values - lax.optimization_barrier(jnp.mean(values, -1, keepdims=True))
    spread = lax.optimization_barrier(jnp.mean(centred * centred, -1, keepdims=True))
    return centred * lax.rsqrt(spread + EPSILON)

def norm_back(inputs, upstream):
    values = inputs.astype(jnp.float32)
    centred = values - lax.optimization_barrier(jnp.mean(values, -1, keepdims=True))
    inv_std = lax.rsqrt(lax.optimization_barrier(jnp.mean(centred * centred, -1, keepdims=True)) + EPSILON)
    normed = centred * inv_std
    return inv_std * (upstream - lax.optimization_barrier(jnp.mean(upstream, -1, keepdims=True)) - normed * lax.optimization_barrier(jnp.mean(upstream * normed, -1, keepdims=True)))

def gelu_back(pre_act, upstream):
    return jax.vjp(lambda inner: jax.nn.gelu(inner, approximate=False), pre_act)[1](upstream)[0]

def head_scores(queries, key_rows):
    return matmul(queries, key_rows.T) * DH ** (-0.5)

def head_forward(queries, key_rows, value_rows):
    scores = head_scores(queries, key_rows)
    row_max = lax.optimization_barrier(jnp.max(scores, -1))
    exp_scores = jnp.exp(scores - row_max[:, None])
    row_sum = lax.optimization_barrier(jnp.sum(exp_scores, -1))
    soft_probs = exp_scores / row_sum[:, None]
    context = matmul(soft_probs.astype(jnp.bfloat16), value_rows).astype(jnp.bfloat16)
    return (context, row_max, row_sum)

def head_backward(queries, key_rows, value_rows, row_max, row_sum, grad_context):
    scores = head_scores(queries, key_rows)
    soft_probs = jnp.exp(scores - row_max[:, None]) / row_sum[:, None]
    grad_probs = matmul(grad_context, value_rows.T)
    row_delta = lax.optimization_barrier(jnp.sum(soft_probs * grad_probs, -1))
    grad_scores = (soft_probs * (grad_probs - row_delta[:, None]) * DH ** (-0.5)).astype(jnp.bfloat16)
    grad_query = matmul(grad_scores, key_rows)
    grad_key = matmul(grad_scores.T, queries)
    grad_value = matmul(soft_probs.astype(jnp.bfloat16).T, grad_context)
    return (grad_query, grad_key, grad_value)

def reference(pixels, valid_mask, var_ids, embed_weight, var_table, agg_query, agg_key, agg_value, agg_out, pos_embed, w_qkv, w_out, w_up, w_down, cotangent):
    block = math.gcd(PATCHES, 256)
    block_count = PATCHES // block
    table_rows = var_table[var_ids].astype(jnp.float32)
    key_dirs = jnp.einsum('dhj,hj->dh', agg_key.astype(jnp.float32).reshape(D, H, DH), agg_query.reshape(H, DH), precision=HIGHEST).astype(jnp.bfloat16)
    mask_float = valid_mask.astype(jnp.float32)[:, None, None]
    value_heads = agg_value.astype(jnp.float32).reshape(D, H, DH)
    pixel_blocks = pixels.reshape(V, PIX, block_count, block).transpose(2, 0, 1, 3)
    pos_blocks = pos_embed.reshape(block_count, block, D)

    def aggregate(pieces):
        pixel_block, pos_block = pieces
        raw_embed = jnp.einsum('vcp,vcd->vpd', pixel_block.astype(jnp.float32), embed_weight.astype(jnp.float32), precision=HIGHEST)
        embedded = (raw_embed + table_rows[:, None, :]).astype(jnp.bfloat16)
        embed_wide = embedded.astype(jnp.float32)
        scores = jnp.einsum('vpd,dh->vph', embed_wide, key_dirs.astype(jnp.float32), precision=HIGHEST) * DH ** (-0.5)
        floored = jnp.where(mask_float > 0, scores, MASK_FLOOR)
        weights = jnp.exp(floored - lax.optimization_barrier(jnp.max(floored, 0))) * mask_float
        shares = weights / lax.optimization_barrier(jnp.sum(weights, 0))
        pooled = jnp.einsum('vph,vpd->phd', shares, embed_wide, precision=HIGHEST)
        mixed_rows = jnp.einsum('phd,dhj->phj', pooled, value_heads, precision=HIGHEST).reshape(block, D).astype(jnp.bfloat16)
        return (matmul(mixed_rows, agg_out) + pos_block.astype(jnp.float32)).astype(jnp.bfloat16)
    tokens = lax.map(aggregate, (pixel_blocks, pos_blocks)).reshape(PATCHES, D)
    normed_in = layer_norm(tokens).astype(jnp.bfloat16)
    qkv_flat = w_qkv.reshape(D, 3 * D)
    qkv = matmul(normed_in, qkv_flat).astype(jnp.bfloat16).reshape(PATCHES, 3, H, DH)
    head_parts = qkv.transpose(1, 2, 0, 3)
    context, row_max, row_sum = lax.map(lambda parts: head_forward(*parts), (head_parts[0], head_parts[1], head_parts[2]))
    context_rows = context.transpose(1, 0, 2).reshape(PATCHES, D)
    middle = (tokens.astype(jnp.float32) + matmul(context_rows, w_out)).astype(jnp.bfloat16)
    normed_mid = layer_norm(middle).astype(jnp.bfloat16)
    pre_act = matmul(normed_mid, w_up)
    activated = jax.nn.gelu(pre_act, approximate=False).astype(jnp.bfloat16)
    layer_out = (middle.astype(jnp.float32) + matmul(activated, w_down)).astype(jnp.bfloat16)
    grad_down = matmul(activated.T, cotangent)
    grad_pre = gelu_back(pre_act, matmul(cotangent, w_down.T)).astype(jnp.bfloat16)
    grad_up = matmul(normed_mid.T, grad_pre)
    grad_middle = (cotangent.astype(jnp.float32) + norm_back(middle, matmul(grad_pre, w_up.T))).astype(jnp.bfloat16)
    grad_out = matmul(context_rows.T, grad_middle)
    grad_context = matmul(grad_middle, w_out.T).astype(jnp.bfloat16)
    grad_heads = grad_context.reshape(PATCHES, H, DH).transpose(1, 0, 2)
    grad_query, grad_key, grad_value = lax.map(lambda parts: head_backward(*parts), (head_parts[0], head_parts[1], head_parts[2], row_max, row_sum, grad_heads))
    grad_stack = jnp.stack([grad_query, grad_key, grad_value], 0).astype(jnp.bfloat16)
    grad_qkv_rows = grad_stack.transpose(2, 0, 1, 3).reshape(PATCHES, 3 * D)
    grad_qkv = matmul(normed_in.T, grad_qkv_rows).reshape(D, 3, D)
    grad_in = matmul(grad_qkv_rows, qkv_flat.T)
    grad_tokens = (grad_middle.astype(jnp.float32) + norm_back(tokens, grad_in)).astype(jnp.bfloat16)
    return (layer_out, grad_tokens, grad_qkv, grad_out, grad_up, grad_down)
```

```python
import functools
import jax
import jax.numpy as jnp
from jax import lax
from jax.experimental import pallas as pl
from jax.experimental.pallas import tpu as pltpu
from jax.sharding import PartitionSpec as P

D = 1024
H = 16
DH = 64
EPSILON = 1e-05
MASK_FLOOR = -1e30
HIGHEST = lax.Precision.HIGHEST
MESH = pl.DeviceIdType.MESH
VMEM = pl.BlockSpec(memory_space=pltpu.VMEM)


def matmul(left, right):
    return jnp.dot(left, right, preferred_element_type=jnp.float32)


def transfer_kernel(axis, n, count, spread, *refs):
    ins, outs = refs[:count], refs[count : 2 * count]
    lands = refs[2 * count : 3 * count]
    send_sem, recv_sem = refs[3 * count :]
    me = lax.axis_index(axis)
    barrier = pltpu.get_barrier_semaphore()

    def greet(d, carry):
        pl.semaphore_signal(
            barrier, inc=1, device_id={axis: lax.rem(me + d, n)}, device_id_type=MESH
        )
        return carry

    lax.fori_loop(1, n, greet, 0)
    pl.semaphore_wait(barrier, n - 1)

    def send(d, carry):
        there = lax.rem(me + d, n)
        for k in range(count):
            pltpu.make_async_remote_copy(
                src_ref=ins[k].at[there] if spread else ins[k],
                dst_ref=lands[k].at[d - 1],
                send_sem=send_sem.at[k],
                recv_sem=recv_sem.at[k],
                device_id={axis: there},
                device_id_type=MESH,
            ).start()
        return carry

    lax.fori_loop(1, n, send, 0)
    for k in range(count):
        outs[k][me] = ins[k][me] if spread else ins[k][...]
    for k in range(count):
        pltpu.make_async_copy(lands[k], lands[k], recv_sem.at[k]).wait()

    def place(d, carry):
        for k in range(count):
            outs[k][lax.rem(me - d + n, n)] = lands[k][d - 1]
        return carry

    lax.fori_loop(1, n, place, 0)
    for k in range(count):
        pltpu.make_async_copy(lands[k], lands[k], send_sem.at[k]).wait()


def transfer(axis, n, number, spread, *arrays):
    blocks = [a.shape[1:] if spread else a.shape for a in arrays]
    count = len(arrays)
    return pl.pallas_call(
        functools.partial(transfer_kernel, axis, n, count, spread),
        out_shape=[
            jax.ShapeDtypeStruct((n,) + b, a.dtype) for a, b in zip(arrays, blocks)
        ],
        in_specs=[VMEM] * count,
        out_specs=[VMEM] * count,
        scratch_shapes=[pltpu.VMEM((n - 1,) + b, a.dtype) for a, b in zip(arrays, blocks)]
        + [pltpu.SemaphoreType.DMA((count,)), pltpu.SemaphoreType.DMA((count,))],
        compiler_params=pltpu.CompilerParams(
            collective_id=number, has_side_effects=True, vmem_limit_bytes=48 * 2**20
        ),
        name="transfer_%d" % number,
    )(*arrays)


def gather(axis, n, number, *arrays):
    return transfer(axis, n, number, False, *arrays)


def exchange(axis, n, number, *arrays):
    return transfer(axis, n, number, True, *arrays)


def layer_norm(inputs):
    values = inputs.astype(jnp.float32)
    centred = values - jnp.mean(values, -1, keepdims=True)
    spread = jnp.mean(centred * centred, -1, keepdims=True)
    return centred * lax.rsqrt(spread + EPSILON)


def norm_back(inputs, upstream):
    values = inputs.astype(jnp.float32)
    centred = values - jnp.mean(values, -1, keepdims=True)
    inv_std = lax.rsqrt(jnp.mean(centred * centred, -1, keepdims=True) + EPSILON)
    normed = centred * inv_std
    return inv_std * (
        upstream
        - jnp.mean(upstream, -1, keepdims=True)
        - normed * jnp.mean(upstream * normed, -1, keepdims=True)
    )


def gelu_back(pre_act, upstream):
    return jax.vjp(lambda inner: jax.nn.gelu(inner, approximate=False), pre_act)[1](upstream)[0]


def shards(nvar, nspace, pixels, valid_mask, var_ids, embed_weight, var_table, agg_query, agg_key,
           agg_value, agg_out, pos_embed, w_qkv, w_out, w_up, w_down, cotangent):
    bf16, f32 = jnp.bfloat16, jnp.float32
    at = lax.axis_index("var")
    slots, rows = pixels.shape[0], pixels.shape[2]
    part = rows // nvar
    key_part = jnp.einsum(
        "dhj,hj->dh", agg_key.astype(f32).reshape(agg_key.shape[0], H, DH),
        agg_query.reshape(H, DH), precision=HIGHEST).astype(bf16)
    key_dirs, = gather("space", nspace, 0, jnp.pad(key_part, ((0, 0), (0, 128 - H))))
    key_dirs = key_dirs.reshape(D, 128)[:, :H]
    raw_embed = jnp.einsum("vcp,vcd->vpd", pixels, embed_weight, preferred_element_type=f32)
    one_hot = (var_ids[:, None] == jnp.arange(var_table.shape[0], dtype=jnp.int32)[None, :]).astype(bf16)
    embedded = (raw_embed + matmul(one_hot, var_table)[:, None, :]).astype(bf16)
    scores = jnp.einsum("vpd,dh->vph", embedded, key_dirs, preferred_element_type=f32) * DH ** (-0.5)
    mask = valid_mask.astype(f32)[:, None, None]
    floored = jnp.where(mask > 0, scores, MASK_FLOOR)
    top = jnp.max(floored, 0)
    weights = jnp.exp(floored - top) * mask
    total = jnp.sum(weights, 0)
    shares = weights / total
    level = top + jnp.log(total)
    values = jnp.einsum("vpd,de->vpe", embedded, agg_value, preferred_element_type=f32)
    pooled = jnp.sum(jnp.repeat(shares, DH, axis=2) * values, 0)
    pieces, levels = exchange(
        "var", nvar, 1, pooled.astype(bf16).reshape(nvar, part, D),
        jnp.pad(level, ((0, 0), (0, 128 - H))).reshape(nvar, part, 128))
    levels = levels[:, :, :H]
    lifts = jnp.exp(levels - jnp.max(levels, 0))
    lifts = lifts / jnp.sum(lifts, 0)
    mixed = jnp.sum(jnp.repeat(lifts, DH, axis=2) * pieces.astype(f32), 0).astype(bf16)
    pos_rows = lax.dynamic_slice_in_dim(pos_embed, at * part, part, 0)
    token_part = (matmul(mixed, agg_out) + pos_rows.astype(f32)).astype(bf16)
    tokens, = gather("var", nvar, 2, token_part)
    tokens = tokens.reshape(rows, D)
    normed_in = layer_norm(tokens).astype(bf16)
    qkv = jnp.einsum("td,dcn->tcn", normed_in, w_qkv, preferred_element_type=f32).astype(bf16)
    queries = qkv[:, 0]
    keys, vals = gather("space", nspace, 3, qkv[:, 1], qkv[:, 2])
    keys = keys.reshape(nspace * rows, 128)
    vals = vals.reshape(nspace * rows, 128)
    heads = [slice(0, 64), slice(64, 128)]
    kept, contexts = [], []
    for h in heads:
        scores_t = lax.dot_general(keys[:, h], queries[:, h], (((1,), (1,)), ((), ())),
                                   preferred_element_type=f32) * DH ** (-0.5)
        exps = jnp.exp(scores_t - jnp.max(scores_t, 0))
        probs = exps / jnp.sum(exps, 0)
        kept.append(probs)
        contexts.append(lax.dot_general(probs.astype(bf16), vals[:, h], (((0,), (0,)), ((), ())),
                                        preferred_element_type=f32).astype(bf16))
    context = jnp.concatenate(contexts, 1)

    def reduce_rows(partial, number):
        arrived, = exchange("var", nvar, number, partial.astype(bf16).reshape(nvar, part, D))
        return jnp.sum(arrived.astype(f32), 0)

    def own(array):
        return lax.dynamic_slice_in_dim(array, at * part, part, 0)

    middle_part = (own(tokens).astype(f32) + reduce_rows(matmul(context, w_out), 4)).astype(bf16)
    middle, = gather("var", nvar, 5, middle_part)
    middle = middle.reshape(rows, D)
    normed_mid = layer_norm(middle).astype(bf16)
    pre_act = matmul(normed_mid, w_up)
    activated = jax.nn.gelu(pre_act, approximate=False).astype(bf16)
    layer_part = (middle_part.astype(f32) + reduce_rows(matmul(activated, w_down), 6)).astype(bf16)
    layer_out, = gather("var", nvar, 7, layer_part)
    layer_out = layer_out.reshape(rows, D)
    grad_down = matmul(activated.T, cotangent)
    grad_pre = gelu_back(pre_act, matmul(cotangent, w_down.T)).astype(bf16)
    grad_up = matmul(normed_mid.T, grad_pre)
    grad_mid_norm = reduce_rows(matmul(grad_pre, w_up.T), 8)
    grad_mid_part = (own(cotangent).astype(f32) + norm_back(middle_part, grad_mid_norm)).astype(bf16)
    grad_middle, = gather("var", nvar, 9, grad_mid_part)
    grad_middle = grad_middle.reshape(rows, D)
    grad_out = matmul(context.T, grad_middle)
    grad_context = matmul(grad_middle, w_out.T).astype(bf16)
    grad_q, grad_k, grad_v = [], [], []
    for h, probs in zip(heads, kept):
        upstream = grad_context[:, h]
        grad_probs = lax.dot_general(vals[:, h], upstream, (((1,), (1,)), ((), ())),
                                     preferred_element_type=f32)
        delta = jnp.sum(probs * grad_probs, 0)
        grad_scores = (probs * (grad_probs - delta) * DH ** (-0.5)).astype(bf16)
        grad_q.append(lax.dot_general(grad_scores, keys[:, h], (((0,), (0,)), ((), ())),
                                      preferred_element_type=f32))
        grad_k.append(matmul(grad_scores, queries[:, h]))
        grad_v.append(matmul(probs.astype(bf16), upstream))
    shape = (nspace, rows, 128)
    k_parts, v_parts = exchange(
        "space", nspace, 10, jnp.concatenate(grad_k, 1).astype(bf16).reshape(shape),
        jnp.concatenate(grad_v, 1).astype(bf16).reshape(shape))
    grad_rows = jnp.concatenate(
        [jnp.concatenate(grad_q, 1).astype(bf16), jnp.sum(k_parts.astype(f32), 0).astype(bf16),
         jnp.sum(v_parts.astype(f32), 0).astype(bf16)], 1)
    grad_qkv = matmul(normed_in.T, grad_rows)
    grad_in = reduce_rows(lax.dot_general(grad_rows, w_qkv.reshape(D, 384), (((1,), (1,)), ((), ())),
                                          preferred_element_type=f32), 11)
    grad_tok_part = (grad_mid_part.astype(f32) + norm_back(own(tokens), grad_in)).astype(bf16)
    grad_tokens, = gather("var", nvar, 12, grad_tok_part)
    sums = []
    for number, grad in ((13, grad_qkv), (14, grad_out), (15, grad_up), (16, grad_down)):
        shape = (nspace, grad.shape[0] // nspace, grad.shape[1])
        if shape[1] < 16:
            shape = (nspace, 16, grad.shape[0] * grad.shape[1] // nspace // 16)
        arrived, = exchange("space", nspace, number, grad.astype(bf16).reshape(shape))
        sums.append(jnp.sum(arrived.astype(f32), 0).reshape(grad.shape[0] // nspace, grad.shape[1]))
    return (layer_out, grad_tokens.reshape(rows, D), sums[0].reshape(D // nspace, 3, 128),
            sums[1], sums[2], sums[3])


def solution(mesh):
    in_specs = (
        P("var", None, "space"), P("var"), P("var"), P("var", None, None), P(), P(),
        P("space", None), P(), P(), P("space", None), P(None, None, "var"), P("var", None),
        P(None, "var"), P("var", None), P("space", None),
    )
    out_specs = (
        P("space", None), P("space", None), P("space", None, "var"),
        P(("var", "space"), None), P("space", "var"), P(("var", "space"), None),
    )
    body = functools.partial(shards, mesh.shape["var"], mesh.shape["space"])
    return jax.shard_map(body, mesh=mesh, in_specs=in_specs, out_specs=out_specs, check_vma=False)
```

```python
import functools
import jax
import jax.numpy as jnp
from jax import lax
from jax.experimental import pallas as pl
from jax.experimental.pallas import tpu as pltpu
from jax.sharding import PartitionSpec as P

D = 1024
H = 16
DH = 64
V = 96
NV = 8
CHIPS = 16
SLOTS = V // NV
ROWS = 128
PART = ROWS // NV
HID = 512
KEYS = 4096
HALF = KEYS // 2
CHUNK = 512
EPSILON = 1e-05
MASK_FLOOR = -1e30
MESH = pl.DeviceIdType.MESH
bf16, f32 = jnp.bfloat16, jnp.float32
FAR_FIRST = (4, 3, 5, 2, 6, 1, 7)


def nn(a, b):
    return jnp.dot(a, b, preferred_element_type=f32)


def nt(a, b):
    return lax.dot_general(a, b, (((1,), (1,)), ((), ())), preferred_element_type=f32)


def tn(a, b):
    return lax.dot_general(a, b, (((0,), (0,)), ((), ())), preferred_element_type=f32)


def mean(values):
    return jnp.mean(values, -1, keepdims=True)


def layer_norm(inputs):
    values = inputs.astype(f32)
    centred = values - mean(values)
    return centred * lax.rsqrt(mean(centred * centred) + EPSILON)


def norm_back(inputs, upstream):
    values = inputs.astype(f32)
    centred = values - mean(values)
    inv_std = lax.rsqrt(mean(centred * centred) + EPSILON)
    normed = centred * inv_std
    return inv_std * (upstream - mean(upstream) - normed * mean(upstream * normed))


def thirds(wide, lane):
    high = wide.astype(bf16).astype(f32)
    rest = wide - high
    middle = rest.astype(bf16).astype(f32)
    low = rest - middle
    picked = jnp.where(lane < H, high, jnp.where(lane < 2 * H, middle, low))
    return jnp.where(lane < 3 * H, picked, 0.0).astype(bf16)


def iota(shape, dim):
    return lax.broadcasted_iota(jnp.int32, shape, dim)


SCRATCH = dict(
    pixels=((SLOTS, 64, ROWS), bf16),
    embed_w=((SLOTS, 64, D), bf16),
    table=((V, D), bf16),
    agg_key=((32, D), bf16),
    agg_value=((D, D), bf16),
    agg_out=((D, D), bf16),
    pos=((ROWS, D), bf16),
    w_qkv=((D, 384), bf16),
    w_out=((ROWS, D), bf16),
    w_up=((D, HID), bf16),
    w_down=((HID, D), bf16),
    cot=((ROWS, D), bf16),
    table_rows=((16, D), f32),
    embedded=((SLOTS * ROWS, D), bf16),
    values=((SLOTS * ROWS, D), f32),
    dirs_part=((32, 128), bf16),
    dirs_land=((2, CHIPS, 32, 128), bf16),
    dirs=((D, 128), bf16),
    scores=((SLOTS * ROWS, 128), f32),
    shares=((SLOTS * ROWS, 128), bf16),
    pooled=((ROWS, D), bf16),
    level=((ROWS, 128), f32),
    pooled_land=((7, PART, D), bf16),
    level_land=((7, PART, 128), f32),
    tokens=((ROWS, D), bf16),
    normed_in=((ROWS, D), bf16),
    keys=((KEYS, 128), bf16),
    vals=((KEYS, 128), bf16),
    q_two=((256, 128), bf16),
    d_two=((256, 128), bf16),
    probs=((KEYS, 256), f32),
    probs_b=((KEYS, 256), bf16),
    grad_probs=((KEYS, 256), f32),
    context=((ROWS, 128), bf16),
    attn=((ROWS, D), bf16),
    attn_land=((7, PART, D), bf16),
    middle=((ROWS, D), bf16),
    normed_mid=((ROWS, D), bf16),
    upstream=((ROWS, HID), f32),
    activated=((ROWS, HID), bf16),
    grad_pre=((ROWS, HID), bf16),
    gmid=((ROWS, D), bf16),
    gmid_land=((7, PART, D), bf16),
    down=((ROWS, D), bf16),
    down_land=((7, PART, D), bf16),
    layer=((ROWS, D), bf16),
    grad_middle=((ROWS, D), bf16),
    gk=((KEYS, 128), bf16),
    gv=((KEYS, 128), bf16),
    gk_sib=((HALF, 128), bf16),
    gv_sib=((HALF, 128), bf16),
    gk_sum=((CHIPS, 128, 128), bf16),
    gv_sum=((CHIPS, 128, 128), bf16),
    gk_land=((CHIPS - 1, 128, 128), bf16),
    gv_land=((CHIPS - 1, 128, 128), bf16),
    grad_rows=((ROWS, 384), bf16),
    gin=((ROWS, D), bf16),
    gin_land=((7, PART, D), bf16),
    grad_tok=((ROWS, D), bf16),
)
WEIGHT_GRADS = dict(down=(16, D), up=(32, HID), out=(16, 256), qkv=(32, 384))
for _name, (_r, _w) in WEIGHT_GRADS.items():
    SCRATCH["wg_part_" + _name] = ((32 * _r, _w), bf16)
    SCRATCH["wg_sib_" + _name] = ((CHIPS, _r, _w), bf16)
    SCRATCH["wg_sum_" + _name] = ((CHIPS, _r, _w), bf16)
    SCRATCH["wg_land_" + _name] = ((CHIPS - 1, _r, _w), bf16)
LOADED = ("agg_key", "pixels", "embed_w", "table", "agg_value", "agg_out", "pos", "w_qkv",
          "w_out", "w_up", "w_down", "cot")
SEMS = 160


class Names:
    pass


def whole_kernel(*refs):
    mask_ref, ids_ref, query_ref = refs[:3]
    hbm = dict(zip(LOADED, refs[3 : 3 + len(LOADED)]))
    at = 3 + len(LOADED)
    layer_ref, gtok_ref, gqkv_ref, gout_ref, gup_ref, gdown_ref = refs[at : at + 6]
    at += 6
    b = Names()
    for name, ref in zip(SCRATCH, refs[at : at + len(SCRATCH)]):
        setattr(b, name, ref)
    load_sem, ss, rs = refs[at + len(SCRATCH) :]

    v = lax.axis_index("var")
    s = lax.axis_index("space")
    core = lax.rem(s, 2)
    chip = s // 2
    cx, cy = chip // 4, lax.rem(chip, 4)
    sib = s + 1 - 2 * core
    own = pl.ds(pl.multiple_of(v * PART, PART), PART)

    def chip_at(dx, dy):
        return lax.rem(cx + dx, 4) * 4 + lax.rem(cy + dy, 4)

    offsets = [(dx, dy) for dx in range(4) for dy in range(4)]
    around = {o: chip_at(*o) for o in offsets}

    used = [0]
    pending = []

    def fresh(n=1):
        used[0] += n
        assert used[0] <= SEMS
        return used[0] - n

    def wait(sem, ref):
        pltpu.make_async_copy(ref, ref, sem).wait()

    def send(src, dst, k, where):
        pltpu.make_async_remote_copy(
            src_ref=src, dst_ref=dst, send_sem=ss.at[k], recv_sem=rs.at[k],
            device_id=where, device_id_type=MESH,
        ).start()

    def to_core(c):
        return {"space": c}

    def same_core(o):
        return {"space": around[o] * 2 + core}

    loads = {}
    for i, name in enumerate(LOADED):
        loads[name] = pltpu.make_async_copy(hbm[name], getattr(b, name), load_sem.at[i])
        loads[name].start()

    def ready(*names):
        for name in names:
            loads[name].wait()

    barrier = pltpu.get_barrier_semaphore()
    for d in range(1, 8):
        pl.semaphore_signal(barrier, inc=1, device_id={"var": lax.rem(v + d, NV)}, device_id_type=MESH)
    for o in offsets[1:]:
        pl.semaphore_signal(barrier, inc=1, device_id=same_core(o), device_id_type=MESH)
    pl.semaphore_signal(barrier, inc=1, device_id=to_core(sib), device_id_type=MESH)

    def z_scatter(src, land):
        k = fresh()
        for d in FAR_FIRST:
            there = lax.rem(v + d, NV)
            send(src.at[pl.ds(pl.multiple_of(there * PART, PART), PART)], land.at[d - 1], k,
                 {"var": there})
        pending.append((k, land))
        return lambda: wait(rs.at[k], land)

    def z_gather(ref):
        k = fresh()
        for d in FAR_FIRST:
            send(ref.at[own], ref.at[own], k, {"var": lax.rem(v + d, NV)})
        pending.append((k, ref.at[pl.ds(0, 7 * PART)]))
        return lambda: wait(rs.at[k], ref.at[pl.ds(0, 7 * PART)])

    def landed(src, land):
        total = src[own].astype(f32)
        for d in range(7):
            total = total + land[d].astype(f32)
        return total

    class Reduce:
        def __init__(self, name):
            self.part = getattr(b, "wg_part_" + name)
            self.sib = getattr(b, "wg_sib_" + name)
            self.sum = getattr(b, "wg_sum_" + name)
            self.land = getattr(b, "wg_land_" + name)
            self.r = WEIGHT_GRADS[name][0]
            self.k = fresh(2)

        def block(self, which, side):
            return pl.ds(pl.multiple_of((2 * which + side) * self.r, self.r), self.r)

        def start(self):
            for i in range(CHIPS):
                send(self.part.at[self.block(i, 1 - core)], self.sib.at[i], self.k, to_core(sib))
            pending.append((self.k, self.sib))

        def spread(self):
            wait(rs.at[self.k], self.sib)

            def add(i, carry):
                self.sum[i] = (self.part[self.block(i, core)].astype(f32)
                               + self.sib[i].astype(f32)).astype(bf16)
                return carry

            lax.fori_loop(0, CHIPS, add, 0)
            for j, o in enumerate(offsets[1:]):
                send(self.sum.at[around[o]], self.land.at[j], self.k + 1, same_core(o))
            pending.append((self.k + 1, self.land))

        def finish(self):
            wait(rs.at[self.k + 1], self.land)
            total = self.part[self.block(chip, core)].astype(f32) + self.sib[chip].astype(f32)
            for j in range(CHIPS - 1):
                total = total + self.land[j].astype(f32)
            return total

    ready("agg_key")
    row, lane = iota((128, D), 0), iota((128, D), 1)
    spots = (lane // DH == lax.rem(row, H)) & (row < 3 * H)
    spread_one = jnp.where(spots, 1.0, 0.0).astype(bf16)
    rest = jnp.where(spots, query_ref[...], 0.0)
    dirs = jnp.zeros((32, 128), f32)
    for _ in range(3):
        piece = rest.astype(bf16)
        dirs = dirs + nt(b.agg_key[...], piece)
        rest = rest - piece.astype(f32)
    b.dirs_part[...] = dirs.astype(bf16)
    b.dirs_land[0, 0] = dirs.astype(bf16)

    pl.semaphore_wait(barrier, 7 + CHIPS - 1 + 1)
    dirs_k = fresh(2)
    for j, o in enumerate(offsets[1:]):
        send(b.dirs_part, b.dirs_land.at[0, j + 1], dirs_k, same_core(o))
    pending.append((dirs_k, b.dirs_land.at[0, pl.ds(1, CHIPS - 1)]))

    ready("table")
    row, lane = iota((16, V), 0), iota((16, V), 1)
    picks = jnp.zeros((16, V), f32)
    for i in range(SLOTS):
        picks = picks + jnp.where((row == i) & (lane == ids_ref[i]), 1.0, 0.0)
    b.table_rows[...] = nn(picks.astype(bf16), b.table[...])
    ready("pixels", "embed_w")

    def embed(i, carry):
        raw = tn(b.pixels[i], b.embed_w[i])
        b.embedded[pl.ds(pl.multiple_of(i * ROWS, ROWS), ROWS)] = (
            raw + b.table_rows[pl.ds(i, 1)]).astype(bf16)
        return carry

    lax.fori_loop(0, SLOTS, embed, 0)
    wait(rs.at[dirs_k], b.dirs_land.at[0, pl.ds(1, CHIPS - 1)])
    send(b.dirs_land.at[0], b.dirs_land.at[1], dirs_k + 1, to_core(sib))
    pending.append((dirs_k + 1, b.dirs_land.at[1]))
    ready("agg_value")

    def value_columns(i, carry):
        columns = pl.ds(pl.multiple_of(i * 256, 256), 256)
        for m in range(2):
            these = pl.ds(m * 768, 768)
            b.values[these, columns] = nn(b.embedded[these], b.agg_value[:, columns])
        return carry

    lax.fori_loop(0, 4, value_columns, 0)
    wait(rs.at[dirs_k + 1], b.dirs_land.at[1])
    for j, o in enumerate(offsets):
        source = lax.rem(cx - o[0] + 4, 4) * 4 + lax.rem(cy - o[1] + 4, 4)
        for side in range(2):
            owner = 2 * source + (core if side == 0 else 1 - core)
            b.dirs[pl.ds(pl.multiple_of(owner * 32, 32), 32)] = b.dirs_land[side, j]

    b.scores[...] = nn(b.embedded[...], b.dirs[...]) * DH ** (-0.5)
    lane = iota((ROWS, 128), 1)
    top = jnp.full((ROWS, 128), MASK_FLOOR, f32)
    for i in range(SLOTS):
        rows = pl.ds(i * ROWS, ROWS)
        top = jnp.maximum(top, jnp.where(mask_ref[i] > 0, b.scores[rows], MASK_FLOOR))
    total = jnp.zeros((ROWS, 128), f32)
    for i in range(SLOTS):
        rows = pl.ds(i * ROWS, ROWS)
        weight = jnp.where(mask_ref[i] > 0, jnp.exp(
            jnp.where(mask_ref[i] > 0, b.scores[rows], MASK_FLOOR) - top), 0.0)
        b.scores[rows] = weight
        total = total + weight
    scale = 1.0 / total
    b.level[...] = top + jnp.log(total)
    for i in range(SLOTS):
        rows = pl.ds(i * ROWS, ROWS)
        b.shares[rows] = thirds(b.scores[rows] * scale, lane)
    for c in range(4):
        columns = slice(c * 256, (c + 1) * 256)
        acc = jnp.zeros((ROWS, 256), f32)
        for i in range(SLOTS):
            rows = pl.ds(i * ROWS, ROWS)
            acc = acc + nn(b.shares[rows], spread_one[:, columns]) * b.values[rows, columns]
        b.pooled[:, columns] = acc.astype(bf16)
    level_in = z_scatter(b.level, b.level_land)
    pooled_in = z_scatter(b.pooled, b.pooled_land)

    ready("w_down", "cot")
    b.upstream[...] = nt(b.cot[...], b.w_down[...])
    ready("agg_out", "pos")
    level_in()
    levels = [b.level[own]] + [b.level_land[d] for d in range(7)]
    top = functools.reduce(jnp.maximum, levels)
    lifts = [jnp.exp(x - top) for x in levels]
    scale = 1.0 / sum(lifts[1:], lifts[0])
    lane = iota((PART, 128), 1)
    lifts = [nn(thirds(x * scale, lane), spread_one) for x in lifts]
    pooled_in()
    mixed = lifts[0] * b.pooled[own].astype(f32)
    for d in range(7):
        mixed = mixed + lifts[d + 1] * b.pooled_land[d].astype(f32)
    b.tokens[own] = (nn(mixed.astype(bf16), b.agg_out[...]) + b.pos[own].astype(f32)).astype(bf16)
    tokens_in = z_gather(b.tokens)
    ready("w_qkv", "w_out", "w_up")
    tokens_in()

    b.normed_in[...] = layer_norm(b.tokens[...]).astype(bf16)
    qkv = nn(b.normed_in[...], b.w_qkv[...]).astype(bf16)
    b.keys[pl.ds(0, ROWS)] = qkv[:, 128:256]
    b.vals[pl.ds(0, ROWS)] = qkv[:, 256:]
    slot = lambda dx, dy, side=0: pl.ds(((side * 4 + dx) * 4 + dy) * ROWS, ROWS)
    first = fresh(12)
    for i in range(1, 4):
        send(b.keys.at[slot(0, 0)], b.keys.at[slot(i, 0)], first + i - 1, same_core((i, 0)))
        send(b.vals.at[slot(0, 0)], b.vals.at[slot(0, i)], first + 2 + i, same_core((0, i)))
    for i in range(1, 4):
        send(b.keys.at[slot(0, 0)], b.keys.at[slot(0, i)], first + 5 + i, same_core((0, i)))
        send(b.vals.at[slot(0, 0)], b.vals.at[slot(i, 0)], first + 8 + i, same_core((i, 0)))
    block = b.keys.at[slot(0, 0)]
    for i in range(12):
        pending.append((first + i, block))
    mine = fresh()
    send(b.keys.at[slot(0, 0)], b.keys.at[slot(0, 0, 1)], mine, to_core(sib))
    send(b.vals.at[slot(0, 0)], b.vals.at[slot(0, 0, 1)], mine, to_core(sib))
    twice = b.keys.at[pl.ds(0, 2 * ROWS)]
    pending.append((mine, twice))
    query = qkv[:, :128] * DH ** (-0.5)
    lane = iota((ROWS, 128), 1)
    zero = jnp.zeros((ROWS, 128), bf16)
    b.q_two[pl.ds(0, ROWS)] = jnp.where(lane < DH, query, zero)
    b.q_two[pl.ds(ROWS, ROWS)] = jnp.where(lane < DH, zero, query)
    second = {}
    for i in range(1, 4):
        wait(rs.at[first + i - 1], block)
        for j in range(1, 4):
            second["k", i, j] = k = fresh()
            send(b.keys.at[slot(i, 0)], b.keys.at[slot(i, j)], k, same_core((0, j)))
        wait(rs.at[first + 2 + i], block)
        for j in range(1, 4):
            second["v", j, i] = k = fresh()
            send(b.vals.at[slot(0, i)], b.vals.at[slot(j, i)], k, same_core((j, 0)))
    for i in range(1, 4):
        wait(rs.at[first + 5 + i], block)
        wait(rs.at[first + 8 + i], block)
    fours = fresh()
    send(b.keys.at[pl.ds(ROWS, 3 * ROWS)], b.keys.at[pl.ds(HALF + ROWS, 3 * ROWS)], fours, to_core(sib))
    send(b.vals.at[pl.ds(ROWS, 3 * ROWS)], b.vals.at[pl.ds(HALF + ROWS, 3 * ROWS)], fours, to_core(sib))
    pending.append((fours, b.keys.at[pl.ds(0, 6 * ROWS)]))
    sides = [fours]
    for i in range(1, 4):
        for j in range(1, 4):
            wait(rs.at[second["k", i, j]], block)
            wait(rs.at[second["v", i, j]], block)
            pending.append((second["k", i, j], block))
            pending.append((second["v", i, j], block))
        k = fresh()
        rows = pl.ds(i * 4 * ROWS, 4 * ROWS)
        over = pl.ds(HALF + i * 4 * ROWS, 4 * ROWS)
        send(b.keys.at[rows], b.keys.at[over], k, to_core(sib))
        send(b.vals.at[rows], b.vals.at[over], k, to_core(sib))
        pending.append((k, b.keys.at[pl.ds(0, 8 * ROWS)]))
        sides.append(k)
    wait(rs.at[mine], twice)
    wait(rs.at[sides[0]], b.keys.at[pl.ds(0, 6 * ROWS)])
    for k in sides[1:]:
        wait(rs.at[k], b.keys.at[pl.ds(0, 8 * ROWS)])

    def chunk(i):
        return pl.ds(pl.multiple_of(i * CHUNK, CHUNK), CHUNK)

    def eights(x):
        return x.reshape(CHUNK // 8, 8, 256)

    def score_step(i, top):
        part = nt(b.keys[chunk(i)], b.q_two[...])
        b.probs[chunk(i)] = part
        return jnp.maximum(top, jnp.max(eights(part), 0))

    top = lax.fori_loop(0, KEYS // CHUNK, score_step, jnp.full((8, 256), -jnp.inf, f32))
    top = jnp.max(top, 0, keepdims=True)

    def exp_step(i, total):
        part = jnp.exp(b.probs[chunk(i)] - top)
        b.probs[chunk(i)] = part
        return total + jnp.sum(eights(part), 0)

    total = lax.fori_loop(0, KEYS // CHUNK, exp_step, jnp.zeros((8, 256), f32))
    scale = 1.0 / jnp.sum(total, 0, keepdims=True)

    def context_step(i, acc):
        part = b.probs[chunk(i)] * scale
        b.probs[chunk(i)] = part
        b.probs_b[chunk(i)] = part.astype(bf16)
        return acc + tn(b.vals[chunk(i)], part.astype(bf16))

    acc = lax.fori_loop(0, KEYS // CHUNK, context_step, jnp.zeros((128, 256), f32))
    tall = iota((128, 128), 0)
    b.context[...] = jnp.where(tall < DH, acc[:, :128], acc[:, 128:]).T.astype(bf16)

    b.attn[...] = nn(b.context[...], b.w_out[...]).astype(bf16)
    attn_in = z_scatter(b.attn, b.attn_land)
    attn_in()
    b.middle[own] = (b.tokens[own].astype(f32) + landed(b.attn, b.attn_land)).astype(bf16)
    middle_in = z_gather(b.middle)
    middle_in()

    b.normed_mid[...] = layer_norm(b.middle[...]).astype(bf16)
    pre = nn(b.normed_mid[...], b.w_up[...])
    half = 0.5 * (1.0 + lax.erf(pre * 0.5 ** 0.5))
    b.activated[...] = (pre * half).astype(bf16)
    slope = half + pre * (jnp.exp(-0.5 * pre * pre) * 0.3989422804014327)
    b.grad_pre[...] = (b.upstream[...] * slope).astype(bf16)
    b.gmid[...] = nt(b.grad_pre[...], b.w_up[...]).astype(bf16)
    gmid_in = z_scatter(b.gmid, b.gmid_land)
    b.down[...] = nn(b.activated[...], b.w_down[...]).astype(bf16)
    down_in = z_scatter(b.down, b.down_land)
    wg = {name: Reduce(name) for name in WEIGHT_GRADS}
    wg["down"].part[...] = tn(b.activated[...], b.cot[...]).astype(bf16)
    wg["down"].start()
    gmid_in()
    b.grad_middle[own] = (b.cot[own].astype(f32) + norm_back(
        b.middle[own], landed(b.gmid, b.gmid_land))).astype(bf16)
    grad_middle_in = z_gather(b.grad_middle)
    wg["up"].part[...] = tn(b.normed_mid[...], b.grad_pre[...]).astype(bf16)
    wg["up"].start()
    wg["down"].spread()
    grad_middle_in()

    grad_context = nt(b.grad_middle[...], b.w_out[...]).astype(bf16)
    lane = iota((ROWS, 128), 1)
    b.d_two[pl.ds(0, ROWS)] = jnp.where(lane < DH, grad_context, zero)
    b.d_two[pl.ds(ROWS, ROWS)] = jnp.where(lane < DH, zero, grad_context)

    def delta_step(i, total):
        part = nt(b.vals[chunk(i)], b.d_two[...])
        b.grad_probs[chunk(i)] = part
        return total + jnp.sum(eights(part * b.probs[chunk(i)]), 0)

    delta = lax.fori_loop(0, KEYS // CHUNK, delta_step, jnp.zeros((8, 256), f32))
    delta = jnp.sum(delta, 0, keepdims=True)

    def back_step(i, acc):
        grad = (b.probs[chunk(i)] * (b.grad_probs[chunk(i)] - delta)).astype(bf16)
        b.gk[chunk(i)] = nn(grad, b.q_two[...]).astype(bf16)
        b.gv[chunk(i)] = nn(b.probs_b[chunk(i)], b.d_two[...]).astype(bf16)
        return acc + tn(b.keys[chunk(i)], grad)

    halves = KEYS // CHUNK // 2
    acc = lax.fori_loop(halves, 2 * halves, back_step, jnp.zeros((128, 256), f32))
    kv_k = fresh(2)
    send(b.gk.at[pl.ds(HALF, HALF)], b.gk_sib, kv_k, to_core(sib))
    send(b.gv.at[pl.ds(HALF, HALF)], b.gv_sib, kv_k, to_core(sib))
    pending.append((kv_k, b.gk))
    acc = lax.fori_loop(0, halves, back_step, acc)
    wait(rs.at[kv_k], b.gk)

    def pair_step(i, carry):
        rows = pl.ds(pl.multiple_of(i * ROWS, ROWS), ROWS)
        b.gk_sum[i] = (b.gk[rows].astype(f32) + b.gk_sib[rows].astype(f32)).astype(bf16)
        b.gv_sum[i] = (b.gv[rows].astype(f32) + b.gv_sib[rows].astype(f32)).astype(bf16)
        return carry

    lax.fori_loop(0, CHIPS, pair_step, 0)
    for j, o in enumerate(offsets):
        if j:
            back = same_core(((4 - o[0]) % 4, (4 - o[1]) % 4))
            send(b.gk_sum.at[j], b.gk_land.at[j - 1], kv_k + 1, back)
            send(b.gv_sum.at[j], b.gv_land.at[j - 1], kv_k + 1, back)
    both = b.gk.at[pl.ds(0, 2 * (CHIPS - 1) * ROWS)]
    pending.append((kv_k + 1, both))

    grad_query = jnp.where(tall < DH, acc[:, :128], acc[:, 128:]).T * DH ** (-0.5)
    b.grad_rows[:, :128] = grad_query.astype(bf16)
    down_in()
    b.layer[own] = (b.middle[own].astype(f32) + landed(b.down, b.down_land)).astype(bf16)
    layer_in = z_gather(b.layer)
    wg["up"].spread()
    row, lane = iota((128, 512), 0), iota((128, 512), 1)
    total = jnp.zeros((512, 256), f32)
    for q in range(4):
        pick = (lane // 16 == row // 4) & (lax.rem(lane, 16) == q * 4 + lax.rem(row, 4))
        picked = nn(b.context[...], jnp.where(pick, 1.0, 0.0).astype(bf16)).astype(bf16)
        total = total + tn(picked, b.grad_middle[:, q * 256 : (q + 1) * 256])
    wg["out"].part[...] = total.astype(bf16)
    wg["out"].start()
    layer_in()
    layer_ref[...] = b.layer[...]
    gdown_ref[...] = wg["down"].finish()
    wg["out"].spread()

    wait(rs.at[kv_k + 1], both)
    for c, part, other, land in ((1, b.gk, b.gk_sib, b.gk_land), (2, b.gv, b.gv_sib, b.gv_land)):
        rows = pl.ds(0, ROWS)
        total = part[rows].astype(f32) + other[rows].astype(f32)
        for j in range(CHIPS - 1):
            total = total + land[j].astype(f32)
        b.grad_rows[:, c * 128 : (c + 1) * 128] = total.astype(bf16)

    b.gin[...] = nt(b.grad_rows[...], b.w_qkv[...]).astype(bf16)
    gin_in = z_scatter(b.gin, b.gin_land)
    wg["qkv"].part[...] = tn(b.normed_in[...], b.grad_rows[...]).astype(bf16)
    wg["qkv"].start()
    wg["qkv"].spread()
    gin_in()
    b.grad_tok[own] = (b.grad_middle[own].astype(f32) + norm_back(
        b.tokens[own], landed(b.gin, b.gin_land))).astype(bf16)
    grad_tok_in = z_gather(b.grad_tok)
    gup_ref[...] = wg["up"].finish()
    total = wg["out"].finish()
    for q in range(4):
        gout_ref[:, q * 256 : (q + 1) * 256] = total[q * 4 : (q + 1) * 4]
    total = wg["qkv"].finish()
    for c in range(3):
        gqkv_ref[:, c, :] = total[:, c * 128 : (c + 1) * 128]
    grad_tok_in()
    gtok_ref[...] = b.grad_tok[...]
    for k, ref in pending:
        wait(ss.at[k], ref)


def shards(pixels, valid_mask, var_ids, embed_weight, var_table, agg_query, agg_key,
           agg_value, agg_out, pos_embed, w_qkv, w_out, w_up, w_down, cotangent):
    in_vmem = pl.BlockSpec(memory_space=pltpu.VMEM)
    in_smem = pl.BlockSpec(memory_space=pltpu.SMEM)
    anywhere = pl.BlockSpec(memory_space=pl.ANY)
    big = (agg_key, pixels, embed_weight, var_table, agg_value, agg_out, pos_embed,
           w_qkv.reshape(D, 384), w_out, w_up, w_down, cotangent)
    shape = jax.ShapeDtypeStruct
    return tuple(pl.pallas_call(
        whole_kernel,
        out_shape=[shape((ROWS, D), bf16), shape((ROWS, D), bf16), shape((32, 3, 128), f32),
                   shape((4, D), f32), shape((32, HID), f32), shape((16, D), f32)],
        in_specs=[in_smem, in_smem, in_vmem] + [anywhere] * len(big),
        out_specs=[in_vmem] * 6,
        scratch_shapes=[pltpu.VMEM(*spec) for spec in SCRATCH.values()]
        + [pltpu.SemaphoreType.DMA((len(LOADED),)), pltpu.SemaphoreType.DMA((SEMS,)),
           pltpu.SemaphoreType.DMA((SEMS,))],
        compiler_params=pltpu.CompilerParams(
            collective_id=0, has_side_effects=True, vmem_limit_bytes=60 * 2**20),
        name="whole",
    )(valid_mask, var_ids, agg_query.reshape(1, D), *big))


def solution(mesh):
    in_specs = (
        P("var", None, "space"), P("var"), P("var"), P("var", None, None), P(), P(),
        P("space", None), P(), P(), P("space", None), P(None, None, "var"), P("var", None),
        P(None, "var"), P("var", None), P("space", None),
    )
    out_specs = (
        P("space", None), P("space", None), P("space", None, "var"),
        P(("var", "space"), None), P("space", "var"), P(("var", "space"), None),
    )
    return jax.shard_map(shards, mesh=mesh, in_specs=in_specs, out_specs=out_specs, check_vma=False)
```

```python
import functools
import jax
import jax.numpy as jnp
from jax import lax
from jax.experimental import pallas as pl
from jax.experimental.pallas import tpu as pltpu
from jax.sharding import PartitionSpec as P

D = 1024
H = 16
DH = 64
V = 96
NV = 8
CHIPS = 16
SLOTS = V // NV
ROWS = 128
PART = ROWS // NV
HID = 512
RING = 4
TEAM = 8
KEYS = RING * ROWS
ASKED = 2 * TEAM * ROWS
CHUNK = 128
EPSILON = 1e-05
MASK_FLOOR = -1e30
MESH = pl.DeviceIdType.MESH
bf16, f32 = jnp.bfloat16, jnp.float32
FAR_FIRST = (4, 3, 5, 2, 6, 1, 7)


def nn(a, b):
    return jnp.dot(a, b, preferred_element_type=f32)


def nt(a, b):
    return lax.dot_general(a, b, (((1,), (1,)), ((), ())), preferred_element_type=f32)


def tn(a, b):
    return lax.dot_general(a, b, (((0,), (0,)), ((), ())), preferred_element_type=f32)


def mean(values):
    return jnp.mean(values, -1, keepdims=True)


def layer_norm(inputs):
    values = inputs.astype(f32)
    centred = values - mean(values)
    return centred * lax.rsqrt(mean(centred * centred) + EPSILON)


def norm_back(inputs, upstream):
    values = inputs.astype(f32)
    centred = values - mean(values)
    inv_std = lax.rsqrt(mean(centred * centred) + EPSILON)
    normed = centred * inv_std
    return inv_std * (upstream - mean(upstream) - normed * mean(upstream * normed))


def thirds(wide, lane):
    high = wide.astype(bf16).astype(f32)
    rest = wide - high
    middle = rest.astype(bf16).astype(f32)
    low = rest - middle
    picked = jnp.where(lane < H, high, jnp.where(lane < 2 * H, middle, low))
    return jnp.where(lane < 3 * H, picked, 0.0).astype(bf16)


def iota(shape, dim):
    return lax.broadcasted_iota(jnp.int32, shape, dim)


SCRATCH = dict(
    pixels=((SLOTS, 64, ROWS), bf16),
    embed_w=((SLOTS, 64, D), bf16),
    table=((V, D), bf16),
    agg_key=((32, D), bf16),
    agg_value=((D, D), bf16),
    agg_out=((D, D), bf16),
    pos=((ROWS, D), bf16),
    w_qkv=((3, D, 128), bf16),
    w_out=((ROWS, D), bf16),
    w_up=((D, HID), bf16),
    w_down=((HID, D), bf16),
    cot=((ROWS, D), bf16),
    table_rows=((16, D), f32),
    embedded=((SLOTS * ROWS, D), bf16),
    values=((SLOTS * ROWS, D), f32),
    dirs_part=((32, 128), bf16),
    dirs_land=((2, CHIPS, 32, 128), bf16),
    dirs=((D, 128), bf16),
    scores=((SLOTS * ROWS, 128), f32),
    shares=((SLOTS * ROWS, 128), bf16),
    pooled=((ROWS, D), bf16),
    level=((ROWS, 128), f32),
    pooled_land=((7, PART, D), bf16),
    level_land=((7, PART, 128), f32),
    tokens=((ROWS, D), bf16),
    normed_in=((ROWS, D), bf16),
    keys=((KEYS, 128), bf16),
    vals=((KEYS, 128), bf16),
    asked=((TEAM, ROWS, 128), bf16),
    q_two=((ASKED, 128), bf16),
    graded=((TEAM, 128, ROWS), bf16),
    d_two=((ASKED, 128), bf16),
    probs=((KEYS, ASKED), f32),
    probs_b=((KEYS, ASKED), bf16),
    grad_probs=((KEYS, ASKED), f32),
    spans=((TEAM, 2 * TEAM, 128), f32),
    deltas=((TEAM, 2 * TEAM, 128), f32),
    flat=((2, 2 * TEAM, 128), f32),
    shared=((TEAM, 128, ROWS), bf16),
    shared_land=((TEAM, 128, ROWS), bf16),
    context=((ROWS, 128), bf16),
    attn=((ROWS, D), bf16),
    attn_land=((7, PART, D), bf16),
    middle=((ROWS, D), bf16),
    normed_mid=((ROWS, D), bf16),
    upstream=((ROWS, HID), f32),
    activated=((ROWS, HID), bf16),
    grad_pre=((ROWS, HID), bf16),
    gmid=((ROWS, D), bf16),
    gmid_land=((7, PART, D), bf16),
    down=((ROWS, D), bf16),
    down_land=((7, PART, D), bf16),
    layer=((ROWS, D), bf16),
    grad_middle=((ROWS, D), bf16),
    gq=((TEAM, 128, ROWS), bf16),
    gq_land=((TEAM - 1, 128, ROWS), bf16),
    gk=((RING, ROWS, 128), bf16),
    gv=((RING, ROWS, 128), bf16),
    gk_land=((RING - 1, ROWS, 128), bf16),
    gv_land=((RING - 1, ROWS, 128), bf16),
    grad_rows=((ROWS, 384), bf16),
    gin=((ROWS, D), bf16),
    gin_land=((7, PART, D), bf16),
    grad_tok=((ROWS, D), bf16),
)
WEIGHT_GRADS = dict(down=(16, D), up=(32, HID), out=(16, 256), qkv=(32, 384))
for _name, (_r, _w) in WEIGHT_GRADS.items():
    SCRATCH["wg_part_" + _name] = ((32 * _r, _w), bf16)
    SCRATCH["wg_sib_" + _name] = ((CHIPS, _r, _w), bf16)
    SCRATCH["wg_sum_" + _name] = ((CHIPS, _r, _w), bf16)
    SCRATCH["wg_land_" + _name] = ((CHIPS - 1, _r, _w), bf16)
LOADED = ("agg_key", "pixels", "embed_w", "table", "agg_value", "agg_out", "pos", "w_qkv",
          "w_out", "w_up", "w_down", "cot")
SEMS = 160


class Names:
    pass


def whole_kernel(*refs):
    mask_ref, ids_ref, query_ref = refs[:3]
    hbm = dict(zip(LOADED, refs[3 : 3 + len(LOADED)]))
    at = 3 + len(LOADED)
    layer_ref, gtok_ref, gqkv_ref, gout_ref, gup_ref, gdown_ref = refs[at : at + 6]
    at += 6
    b = Names()
    for name, ref in zip(SCRATCH, refs[at : at + len(SCRATCH)]):
        setattr(b, name, ref)
    load_sem, ss, rs = refs[at + len(SCRATCH) :]

    v = lax.axis_index("var")
    s = lax.axis_index("space")
    core = lax.rem(s, 2)
    chip = s // 2
    cx, cy = chip // 4, lax.rem(chip, 4)
    sib = s + 1 - 2 * core
    own = pl.ds(pl.multiple_of(v * PART, PART), PART)

    def chip_at(dx, dy):
        return lax.rem(cx + dx, 4) * 4 + lax.rem(cy + dy, 4)

    offsets = [(dx, dy) for dx in range(4) for dy in range(4)]
    around = {o: chip_at(*o) for o in offsets}

    used = [0]
    pending = []

    def fresh(n=1):
        used[0] += n
        assert used[0] <= SEMS
        return used[0] - n

    def wait(sem, ref):
        pltpu.make_async_copy(ref, ref, sem).wait()

    def send(src, dst, k, where):
        pltpu.make_async_remote_copy(
            src_ref=src, dst_ref=dst, send_sem=ss.at[k], recv_sem=rs.at[k],
            device_id=where, device_id_type=MESH,
        ).start()

    def to_core(c):
        return {"space": c}

    def same_core(o):
        return {"space": around[o] * 2 + core}

    loads = {}
    for i, name in enumerate(LOADED):
        loads[name] = pltpu.make_async_copy(hbm[name], getattr(b, name), load_sem.at[i])
        loads[name].start()

    def ready(*names):
        for name in names:
            loads[name].wait()

    barrier = pltpu.get_barrier_semaphore()
    for d in range(1, 8):
        pl.semaphore_signal(barrier, inc=1, device_id={"var": lax.rem(v + d, NV)}, device_id_type=MESH)
    for o in offsets[1:]:
        pl.semaphore_signal(barrier, inc=1, device_id=same_core(o), device_id_type=MESH)
    pl.semaphore_signal(barrier, inc=1, device_id=to_core(sib), device_id_type=MESH)
    for d in range(1, RING):
        pl.semaphore_signal(barrier, inc=1, device_id=to_core(around[0, d] * 2 + 1 - core), device_id_type=MESH)

    def z_scatter(src, land):
        k = fresh()
        for d in FAR_FIRST:
            there = lax.rem(v + d, NV)
            send(src.at[pl.ds(pl.multiple_of(there * PART, PART), PART)], land.at[d - 1], k,
                 {"var": there})
        pending.append((k, land))
        return lambda: wait(rs.at[k], land)

    def z_gather(ref):
        k = fresh()
        for d in FAR_FIRST:
            send(ref.at[own], ref.at[own], k, {"var": lax.rem(v + d, NV)})
        pending.append((k, ref.at[pl.ds(0, 7 * PART)]))
        return lambda: wait(rs.at[k], ref.at[pl.ds(0, 7 * PART)])

    def landed(src, land):
        total = src[own].astype(f32)
        for d in range(7):
            total = total + land[d].astype(f32)
        return total

    place = cy * 2 + core
    mates = []
    for d in range(1, RING):
        mates.append((around[0, d] * 2 + core, lax.rem(cy + d, 4) * 2 + core))
        mates.append((around[0, d] * 2 + 1 - core, lax.rem(cy + d, 4) * 2 + 1 - core))
    mates.append((sib, cy * 2 + 1 - core))
    ring = [(same_core((d, 0)), lax.rem(cx + d, 4)) for d in range(1, RING)]

    def team_gather(ref):
        k = fresh()
        for to, _ in mates:
            send(ref.at[place], ref.at[place], k, to_core(to))
        seven = ref.at[pl.ds(0, TEAM - 1)]
        pending.append((k, seven))
        return lambda: wait(rs.at[k], seven)

    def team_scatter(src, land):
        k = fresh()
        for j, (to, t) in enumerate(mates):
            send(src.at[t], land.at[j], k, to_core(to))
        seven = land.at[pl.ds(0, TEAM - 1)]
        pending.append((k, seven))
        return lambda: wait(rs.at[k], seven)

    def ring_gather(ref):
        k = fresh()
        rows = pl.ds(pl.multiple_of(cx * ROWS, ROWS), ROWS)
        for to, _ in ring:
            send(ref.at[rows], ref.at[rows], k, to)
        three = ref.at[pl.ds(0, 3 * ROWS)]
        pending.append((k, three))
        return lambda: wait(rs.at[k], three)

    def ring_scatter(src, land):
        k = fresh()
        for j, (to, t) in enumerate(ring):
            send(src.at[t], land.at[j], k, to)
        pending.append((k, land))
        return lambda: wait(rs.at[k], land)

    class Reduce:
        def __init__(self, name):
            self.part = getattr(b, "wg_part_" + name)
            self.sib = getattr(b, "wg_sib_" + name)
            self.sum = getattr(b, "wg_sum_" + name)
            self.land = getattr(b, "wg_land_" + name)
            self.r = WEIGHT_GRADS[name][0]
            self.k = fresh(2)

        def block(self, which, side):
            return pl.ds(pl.multiple_of((2 * which + side) * self.r, self.r), self.r)

        def start(self):
            for i in range(CHIPS):
                send(self.part.at[self.block(i, 1 - core)], self.sib.at[i], self.k, to_core(sib))
            pending.append((self.k, self.sib))

        def spread(self):
            wait(rs.at[self.k], self.sib)

            def add(i, carry):
                self.sum[i] = (self.part[self.block(i, core)].astype(f32)
                               + self.sib[i].astype(f32)).astype(bf16)
                return carry

            lax.fori_loop(0, CHIPS, add, 0)
            for j, o in enumerate(offsets[1:]):
                send(self.sum.at[around[o]], self.land.at[j], self.k + 1, same_core(o))
            pending.append((self.k + 1, self.land))

        def finish(self):
            wait(rs.at[self.k + 1], self.land)
            total = self.part[self.block(chip, core)].astype(f32) + self.sib[chip].astype(f32)
            for j in range(CHIPS - 1):
                total = total + self.land[j].astype(f32)
            return total

    ready("agg_key")
    row, lane = iota((128, D), 0), iota((128, D), 1)
    spots = (lane // DH == lax.rem(row, H)) & (row < 3 * H)
    spread_one = jnp.where(spots, 1.0, 0.0).astype(bf16)
    rest = jnp.where(spots, query_ref[...], 0.0)
    dirs = jnp.zeros((32, 128), f32)
    for _ in range(3):
        piece = rest.astype(bf16)
        dirs = dirs + nt(b.agg_key[...], piece)
        rest = rest - piece.astype(f32)
    b.dirs_part[...] = dirs.astype(bf16)
    b.dirs_land[0, 0] = dirs.astype(bf16)

    pl.semaphore_wait(barrier, 7 + CHIPS - 1 + 1 + RING - 1)
    dirs_k = fresh(2)
    for j, o in enumerate(offsets[1:]):
        send(b.dirs_part, b.dirs_land.at[0, j + 1], dirs_k, same_core(o))
    pending.append((dirs_k, b.dirs_land.at[0, pl.ds(1, CHIPS - 1)]))

    ready("table")
    row, lane = iota((16, V), 0), iota((16, V), 1)
    picks = jnp.zeros((16, V), f32)
    for i in range(SLOTS):
        picks = picks + jnp.where((row == i) & (lane == ids_ref[i]), 1.0, 0.0)
    b.table_rows[...] = nn(picks.astype(bf16), b.table[...])
    ready("pixels", "embed_w")

    def embed(i, carry):
        raw = tn(b.pixels[i], b.embed_w[i])
        b.embedded[pl.ds(pl.multiple_of(i * ROWS, ROWS), ROWS)] = (
            raw + b.table_rows[pl.ds(i, 1)]).astype(bf16)
        return carry

    lax.fori_loop(0, SLOTS, embed, 0)
    wait(rs.at[dirs_k], b.dirs_land.at[0, pl.ds(1, CHIPS - 1)])
    send(b.dirs_land.at[0], b.dirs_land.at[1], dirs_k + 1, to_core(sib))
    pending.append((dirs_k + 1, b.dirs_land.at[1]))
    ready("agg_value")

    def value_columns(i, carry):
        columns = pl.ds(pl.multiple_of(i * 256, 256), 256)
        for m in range(2):
            these = pl.ds(m * 768, 768)
            b.values[these, columns] = nn(b.embedded[these], b.agg_value[:, columns])
        return carry

    lax.fori_loop(0, 4, value_columns, 0)
    wait(rs.at[dirs_k + 1], b.dirs_land.at[1])
    for j, o in enumerate(offsets):
        source = lax.rem(cx - o[0] + 4, 4) * 4 + lax.rem(cy - o[1] + 4, 4)
        for side in range(2):
            owner = 2 * source + (core if side == 0 else 1 - core)
            b.dirs[pl.ds(pl.multiple_of(owner * 32, 32), 32)] = b.dirs_land[side, j]

    b.scores[...] = nn(b.embedded[...], b.dirs[...]) * DH ** (-0.5)
    lane = iota((ROWS, 128), 1)
    top = jnp.full((ROWS, 128), MASK_FLOOR, f32)
    for i in range(SLOTS):
        rows = pl.ds(i * ROWS, ROWS)
        top = jnp.maximum(top, jnp.where(mask_ref[i] > 0, b.scores[rows], MASK_FLOOR))
    total = jnp.zeros((ROWS, 128), f32)
    for i in range(SLOTS):
        rows = pl.ds(i * ROWS, ROWS)
        weight = jnp.where(mask_ref[i] > 0, jnp.exp(
            jnp.where(mask_ref[i] > 0, b.scores[rows], MASK_FLOOR) - top), 0.0)
        b.scores[rows] = weight
        total = total + weight
    scale = 1.0 / total
    b.level[...] = top + jnp.log(total)
    for i in range(SLOTS):
        rows = pl.ds(i * ROWS, ROWS)
        b.shares[rows] = thirds(b.scores[rows] * scale, lane)
    for c in range(4):
        columns = slice(c * 256, (c + 1) * 256)
        acc = jnp.zeros((ROWS, 256), f32)
        for i in range(SLOTS):
            rows = pl.ds(i * ROWS, ROWS)
            acc = acc + nn(b.shares[rows], spread_one[:, columns]) * b.values[rows, columns]
        b.pooled[:, columns] = acc.astype(bf16)
    level_in = z_scatter(b.level, b.level_land)
    pooled_in = z_scatter(b.pooled, b.pooled_land)

    ready("w_down", "cot")
    b.upstream[...] = nt(b.cot[...], b.w_down[...])
    ready("agg_out", "pos")
    level_in()
    levels = [b.level[own]] + [b.level_land[d] for d in range(7)]
    top = functools.reduce(jnp.maximum, levels)
    lifts = [jnp.exp(x - top) for x in levels]
    scale = 1.0 / sum(lifts[1:], lifts[0])
    lane = iota((PART, 128), 1)
    lifts = [nn(thirds(x * scale, lane), spread_one) for x in lifts]
    pooled_in()
    mixed = lifts[0] * b.pooled[own].astype(f32)
    for d in range(7):
        mixed = mixed + lifts[d + 1] * b.pooled_land[d].astype(f32)
    b.tokens[own] = (nn(mixed.astype(bf16), b.agg_out[...]) + b.pos[own].astype(f32)).astype(bf16)
    tokens_in = z_gather(b.tokens)
    ready("w_qkv", "w_out", "w_up")
    tokens_in()

    b.normed_in[...] = layer_norm(b.tokens[...]).astype(bf16)
    mine = pl.ds(pl.multiple_of(cx * ROWS, ROWS), ROWS)
    b.asked[place] = nn(b.normed_in[...], b.w_qkv[0]).astype(bf16) * DH ** (-0.5)
    asked_in = team_gather(b.asked)
    b.keys[mine] = nn(b.normed_in[...], b.w_qkv[1]).astype(bf16)
    keys_in = ring_gather(b.keys)
    b.vals[mine] = nn(b.normed_in[...], b.w_qkv[2]).astype(bf16)
    vals_in = ring_gather(b.vals)

    def chunk(i):
        return pl.ds(pl.multiple_of(i * CHUNK, CHUNK), CHUNK)

    def eights(x):
        return x.reshape(CHUNK // 8, 8, ASKED)

    def stretch(ref, t):
        return jnp.concatenate([ref[t, pl.ds(r, 1), :] for r in range(2 * TEAM)], 1)

    lane = iota((ROWS, 128), 1)
    zero = jnp.zeros((ROWS, 128), bf16)

    def two(ref, block):
        for t in range(TEAM):
            ref[pl.ds(t * ROWS, ROWS)] = jnp.where(lane < DH, block(t), zero)
            ref[pl.ds((TEAM + t) * ROWS, ROWS)] = jnp.where(lane < DH, zero, block(t))

    asked_in()
    two(b.q_two, lambda t: b.asked[t])
    keys_in()
    steps = KEYS // CHUNK

    def score_step(i, top):
        part = nt(b.keys[chunk(i)], b.q_two[...])
        b.probs[chunk(i)] = part
        return jnp.maximum(top, jnp.max(eights(part), 0))

    top = lax.fori_loop(0, steps, score_step, jnp.full((8, ASKED), -jnp.inf, f32))
    top = jnp.max(top, 0, keepdims=True)

    def exp_step(i, total):
        part = jnp.exp(b.probs[chunk(i)] - top)
        b.probs[chunk(i)] = part
        b.probs_b[chunk(i)] = part.astype(bf16)
        return total + jnp.sum(eights(part), 0)

    total = lax.fori_loop(0, steps, exp_step, jnp.zeros((8, ASKED), f32))
    total = jnp.sum(total, 0, keepdims=True)
    span = top + jnp.log(total)
    for r in range(2 * TEAM):
        b.spans[place, pl.ds(r, 1), :] = span[:, r * 128 : (r + 1) * 128]
    spans_in = team_gather(b.spans)
    vals_in()
    scale = 1.0 / total
    for h in range(2):
        side = slice(h * TEAM * ROWS, (h + 1) * TEAM * ROWS)
        part = tn(b.vals[...], b.probs_b[:, side]) * scale[:, side]
        for t in range(TEAM):
            b.shared[t, h * DH : (h + 1) * DH, :] = (
                part[h * DH : (h + 1) * DH, t * ROWS : (t + 1) * ROWS].astype(bf16))
    shared_in = team_scatter(b.shared, b.shared_land)
    spans_in()
    all_spans = b.spans[...]
    top = jnp.max(all_spans, 0)
    whole_span = top + jnp.log(jnp.sum(jnp.exp(all_spans - top[None]), 0))
    shared_in()

    def lift(t):
        rows = [pl.ds(h * TEAM + place, 1) for h in range(2)]
        each = [jnp.exp(b.spans[t, rows[h], :] - b.flat[0, rows[h], :]) for h in range(2)]
        return jnp.where(iota((128, ROWS), 0) < DH, each[0], each[1])

    b.flat[0] = whole_span
    acc = lift(place) * b.shared[place].astype(f32)
    for j, (_, t) in enumerate(mates):
        back = lax.rem(cy + 4 - (j // 2 + 1), 4) * 2 + (core if j % 2 == 0 else 1 - core)
        acc = acc + lift(back if j < 6 else t) * b.shared_land[j].astype(f32)
    b.context[...] = acc.T.astype(bf16)

    b.attn[...] = nn(b.context[...], b.w_out[...]).astype(bf16)
    attn_in = z_scatter(b.attn, b.attn_land)
    factor = jnp.exp(span - stretch(b.flat, 0)) * scale

    def norm_step(i, carry):
        part = b.probs[chunk(i)] * factor
        b.probs[chunk(i)] = part
        b.probs_b[chunk(i)] = part.astype(bf16)
        return carry

    lax.fori_loop(0, steps, norm_step, 0)
    attn_in()
    b.middle[own] = (b.tokens[own].astype(f32) + landed(b.attn, b.attn_land)).astype(bf16)
    middle_in = z_gather(b.middle)
    middle_in()

    b.normed_mid[...] = layer_norm(b.middle[...]).astype(bf16)
    pre = nn(b.normed_mid[...], b.w_up[...])
    half = 0.5 * (1.0 + lax.erf(pre * 0.5 ** 0.5))
    b.activated[...] = (pre * half).astype(bf16)
    slope = half + pre * (jnp.exp(-0.5 * pre * pre) * 0.3989422804014327)
    b.grad_pre[...] = (b.upstream[...] * slope).astype(bf16)
    b.gmid[...] = nt(b.grad_pre[...], b.w_up[...]).astype(bf16)
    gmid_in = z_scatter(b.gmid, b.gmid_land)
    b.down[...] = nn(b.activated[...], b.w_down[...]).astype(bf16)
    wg = {name: Reduce(name) for name in WEIGHT_GRADS}
    wg["down"].part[...] = tn(b.activated[...], b.cot[...]).astype(bf16)
    wg["down"].start()
    gmid_in()
    b.grad_middle[own] = (b.cot[own].astype(f32) + norm_back(
        b.middle[own], landed(b.gmid, b.gmid_land))).astype(bf16)
    grad_middle_in = z_gather(b.grad_middle)
    wg["up"].part[...] = tn(b.normed_mid[...], b.grad_pre[...]).astype(bf16)
    wg["up"].start()
    wg["down"].spread()
    grad_middle_in()

    b.graded[place] = nt(b.grad_middle[...], b.w_out[...]).astype(bf16)
    graded_in = team_gather(b.graded)
    down_in = z_scatter(b.down, b.down_land)
    row, lane5 = iota((128, 512), 0), iota((128, 512), 1)
    total = jnp.zeros((512, 256), f32)
    for q in range(4):
        pick = (lane5 // 16 == row // 4) & (lax.rem(lane5, 16) == q * 4 + lax.rem(row, 4))
        picked = nn(b.context[...], jnp.where(pick, 1.0, 0.0).astype(bf16)).astype(bf16)
        total = total + tn(picked, b.grad_middle[:, q * 256 : (q + 1) * 256])
    wg["out"].part[...] = total.astype(bf16)
    graded_in()
    two(b.d_two, lambda t: b.graded[t])

    def delta_step(i, total):
        part = nt(b.vals[chunk(i)], b.d_two[...])
        b.grad_probs[chunk(i)] = part
        return total + jnp.sum(eights(part * b.probs[chunk(i)]), 0)

    delta = lax.fori_loop(0, steps, delta_step, jnp.zeros((8, ASKED), f32))
    delta = jnp.sum(delta, 0, keepdims=True)
    for r in range(2 * TEAM):
        b.deltas[place, pl.ds(r, 1), :] = delta[:, r * 128 : (r + 1) * 128]
    deltas_in = team_gather(b.deltas)
    for t in range(RING):
        b.gv[t] = nn(b.probs_b[pl.ds(t * ROWS, ROWS)], b.d_two[...]).astype(bf16)
    gv_in = ring_scatter(b.gv, b.gv_land)
    deltas_in()
    b.flat[1] = jnp.sum(b.deltas[...], 0)
    delta = stretch(b.flat, 1)

    def back_step(i, carry):
        b.probs_b[chunk(i)] = (b.probs[chunk(i)] * (b.grad_probs[chunk(i)] - delta)).astype(bf16)
        return carry

    lax.fori_loop(0, steps, back_step, 0)
    for h in range(2):
        side = slice(h * TEAM * ROWS, (h + 1) * TEAM * ROWS)
        part = tn(b.keys[...], b.probs_b[:, side])
        for t in range(TEAM):
            b.gq[t, h * DH : (h + 1) * DH, :] = (
                part[h * DH : (h + 1) * DH, t * ROWS : (t + 1) * ROWS].astype(bf16))
    gq_in = team_scatter(b.gq, b.gq_land)
    for t in range(RING):
        b.gk[t] = nn(b.probs_b[pl.ds(t * ROWS, ROWS)], b.q_two[...]).astype(bf16)
    gk_in = ring_scatter(b.gk, b.gk_land)

    down_in()
    b.layer[own] = (b.middle[own].astype(f32) + landed(b.down, b.down_land)).astype(bf16)
    layer_in = z_gather(b.layer)
    wg["out"].start()
    gdown_ref[...] = wg["down"].finish()
    for c, part, land, come in ((2, b.gv, b.gv_land, gv_in), (0, b.gq, b.gq_land, gq_in), (1, b.gk, b.gk_land, gk_in)):
        come()
        total = part[cx if c else place].astype(f32)
        for j in range(RING - 1 if c else TEAM - 1):
            total = total + land[j].astype(f32)
        if c == 0:
            total = total.T * DH ** (-0.5)
        b.grad_rows[:, c * 128 : (c + 1) * 128] = total.astype(bf16)

    b.gin[...] = sum(nt(b.grad_rows[:, c * 128 : (c + 1) * 128], b.w_qkv[c]) for c in (1, 2, 0)).astype(bf16)
    gin_in = z_scatter(b.gin, b.gin_land)
    wg["up"].spread()
    wg["out"].spread()
    wg["qkv"].part[...] = tn(b.normed_in[...], b.grad_rows[...]).astype(bf16)
    wg["qkv"].start()
    wg["qkv"].spread()
    gin_in()
    b.grad_tok[own] = (b.grad_middle[own].astype(f32) + norm_back(
        b.tokens[own], landed(b.gin, b.gin_land))).astype(bf16)
    grad_tok_in = z_gather(b.grad_tok)
    gup_ref[...] = wg["up"].finish()
    total = wg["out"].finish()
    for q in range(4):
        gout_ref[:, q * 256 : (q + 1) * 256] = total[q * 4 : (q + 1) * 4]
    total = wg["qkv"].finish()
    for c in range(3):
        gqkv_ref[c] = total[:, c * 128 : (c + 1) * 128]
    grad_tok_in()
    gtok_ref[...] = b.grad_tok[...]
    layer_in()
    layer_ref[...] = b.layer[...]
    for k, ref in pending:
        wait(ss.at[k], ref)


def hand_over(*refs):
    for i in range(6):
        refs[6 + i][...] = refs[i][...]


def shards(pixels, valid_mask, var_ids, embed_weight, var_table, agg_query, agg_key,
           agg_value, agg_out, pos_embed, w_qkv, w_out, w_up, w_down, cotangent):
    in_vmem = pl.BlockSpec(memory_space=pltpu.VMEM)
    in_smem = pl.BlockSpec(memory_space=pltpu.SMEM)
    anywhere = pl.BlockSpec(memory_space=pl.ANY)
    big = (agg_key, pixels, embed_weight, var_table, agg_value, agg_out, pos_embed,
           w_qkv.transpose(1, 0, 2), w_out, w_up, w_down, cotangent)
    shape = jax.ShapeDtypeStruct
    outs = pl.pallas_call(
        whole_kernel,
        out_shape=[shape((ROWS, D), bf16), shape((ROWS, D), bf16), shape((3, 32, 128), f32),
                   shape((4, D), f32), shape((32, HID), f32), shape((16, D), f32)],
        in_specs=[in_smem, in_smem, in_vmem] + [anywhere] * len(big),
        out_specs=[in_vmem] * 6,
        scratch_shapes=[pltpu.VMEM(*spec) for spec in SCRATCH.values()]
        + [pltpu.SemaphoreType.DMA((len(LOADED),)), pltpu.SemaphoreType.DMA((SEMS,)),
           pltpu.SemaphoreType.DMA((SEMS,))],
        compiler_params=pltpu.CompilerParams(
            collective_id=0, has_side_effects=True, vmem_limit_bytes=60 * 2**20),
        name="whole",
    )(valid_mask, var_ids, agg_query.reshape(1, D), *big)
    layer_out, grad_tokens, grad_qkv, grad_out, grad_up, grad_down = pl.pallas_call(
        hand_over,
        out_shape=[shape(x.shape, x.dtype) for x in outs],
        in_specs=[in_vmem] * 6,
        out_specs=[in_vmem] * 6,
        name="hand_over",
    )(*outs)
    return (layer_out, grad_tokens, grad_qkv.transpose(1, 0, 2), grad_out, grad_up, grad_down)


def solution(mesh):
    in_specs = (
        P("var", None, "space"), P("var"), P("var"), P("var", None, None), P(), P(),
        P("space", None), P(), P(), P("space", None), P(None, None, "var"), P("var", None),
        P(None, "var"), P("var", None), P("space", None),
    )
    out_specs = (
        P("space", None), P("space", None), P("space", None, "var"),
        P(("var", "space"), None), P("space", "var"), P(("var", "space"), None),
    )
    return jax.shard_map(shards, mesh=mesh, in_specs=in_specs, out_specs=out_specs, check_vma=False)
```

```python
import functools
import jax
import jax.numpy as jnp
from jax import lax
from jax.experimental import pallas as pl
from jax.experimental.pallas import tpu as pltpu
from jax.sharding import PartitionSpec as P

D = 1024
H = 16
DH = 64
V = 96
NV = 8
CHIPS = 16
SLOTS = V // NV
ROWS = 128
PART = ROWS // NV
HID = 512
RING = 4
TEAM = 8
KEYS = RING * ROWS
ASKED = 2 * TEAM * ROWS
CHUNK = 128
EPSILON = 1e-05
MASK_FLOOR = -1e30
MESH = pl.DeviceIdType.MESH
bf16, f32 = jnp.bfloat16, jnp.float32
FAR_FIRST = (4, 3, 5, 2, 6, 1, 7)


def nn(a, b):
    return jnp.dot(a, b, preferred_element_type=f32)


def nt(a, b):
    return lax.dot_general(a, b, (((1,), (1,)), ((), ())), preferred_element_type=f32)


def tn(a, b):
    return lax.dot_general(a, b, (((0,), (0,)), ((), ())), preferred_element_type=f32)


def mean(values):
    return jnp.mean(values, -1, keepdims=True)


def layer_norm(inputs):
    values = inputs.astype(f32)
    centred = values - mean(values)
    return centred * lax.rsqrt(mean(centred * centred) + EPSILON)


def norm_back(inputs, upstream):
    values = inputs.astype(f32)
    centred = values - mean(values)
    inv_std = lax.rsqrt(mean(centred * centred) + EPSILON)
    normed = centred * inv_std
    return inv_std * (upstream - mean(upstream) - normed * mean(upstream * normed))


def thirds(wide, lane):
    high = wide.astype(bf16).astype(f32)
    rest = wide - high
    middle = rest.astype(bf16).astype(f32)
    low = rest - middle
    picked = jnp.where(lane < H, high, jnp.where(lane < 2 * H, middle, low))
    return jnp.where(lane < 3 * H, picked, 0.0).astype(bf16)


def iota(shape, dim):
    return lax.broadcasted_iota(jnp.int32, shape, dim)


SCRATCH = dict(
    pixels=((SLOTS, 64, ROWS), bf16),
    embed_w=((SLOTS, 64, D), bf16),
    table=((V, D), bf16),
    agg_key=((32, D), bf16),
    agg_value=((D, D), bf16),
    agg_out=((D, D), bf16),
    pos=((ROWS, D), bf16),
    w_qkv=((3, D, 128), bf16),
    w_out=((ROWS, D), bf16),
    w_up=((D, HID), bf16),
    w_down=((HID, D), bf16),
    cot=((ROWS, D), bf16),
    table_rows=((16, D), f32),
    embedded=((SLOTS * ROWS, D), bf16),
    values=((SLOTS * ROWS, D), f32),
    dirs_part=((32, 128), bf16),
    dirs_land=((2, CHIPS, 32, 128), bf16),
    dirs=((D, 128), bf16),
    scores=((SLOTS * ROWS, 128), f32),
    shares=((SLOTS * ROWS, 128), bf16),
    pooled=((ROWS, D), bf16),
    level=((ROWS, 128), f32),
    pooled_land=((2, 7, PART, D // 2), bf16),
    mixed=((ROWS, D), bf16),
    w_full=((NV, RING, 2, PART, D), bf16),
    context_all=((NV, ROWS, 128), bf16),
    level_land=((7, PART, 128), f32),
    tokens=((ROWS, D), bf16),
    normed_in=((ROWS, D), bf16),
    keys=((KEYS, 128), bf16),
    vals=((KEYS, 128), bf16),
    asked=((TEAM, ROWS, 128), bf16),
    q_two=((ASKED, 128), bf16),
    graded=((TEAM, 128, ROWS), bf16),
    d_two=((ASKED, 128), bf16),
    probs=((KEYS, ASKED), f32),
    probs_b=((KEYS, ASKED), bf16),
    grad_probs=((KEYS, ASKED), f32),
    spans=((TEAM, 2 * TEAM, 128), f32),
    deltas=((TEAM, 2 * TEAM, 128), f32),
    flat=((2, 2 * TEAM, 128), f32),
    shared=((TEAM, 128, ROWS), bf16),
    shared_land=((TEAM, 128, ROWS), bf16),
    context=((ROWS, 128), bf16),
    middle=((ROWS, D), bf16),
    normed_mid=((ROWS, D), bf16),
    upstream=((ROWS, HID), f32),
    activated=((ROWS, HID), bf16),
    grad_pre=((ROWS, HID), bf16),
    gmid=((ROWS, D), bf16),
    gmid_land=((2, 7, PART, D // 2), bf16),
    gmid_sum=((ROWS, D), bf16),
    down=((ROWS, D), bf16),
    down_land=((7, PART, D), bf16),
    layer=((ROWS, D), bf16),
    grad_middle=((ROWS, D), bf16),
    gq=((TEAM, 128, ROWS), bf16),
    gq_land=((TEAM - 1, 128, ROWS), bf16),
    gk=((RING, ROWS, 128), bf16),
    gv=((RING, ROWS, 128), bf16),
    gk_land=((RING - 1, ROWS, 128), bf16),
    gv_land=((RING - 1, ROWS, 128), bf16),
    grad_rows=((ROWS, 384), bf16),
    gin=((ROWS, D), bf16),
    gin_land=((2, 7, PART, D // 2), bf16),
    gin_sum=((ROWS, D), bf16),
)
WEIGHT_GRADS = dict(down=(16, D), up=(32, HID), out=(16, 256), qkv=(32, 384))
for _name, (_r, _w) in WEIGHT_GRADS.items():
    SCRATCH["wg_part_" + _name] = ((32 * _r, _w), bf16)
    SCRATCH["wg_sib_" + _name] = ((CHIPS, _r, _w), bf16)
    SCRATCH["wg_sum_" + _name] = ((CHIPS, _r, _w), bf16)
    SCRATCH["wg_land_" + _name] = ((CHIPS - 1, _r, _w), bf16)
LOADED = ("agg_key", "w_out", "table", "pixels", "embed_w", "agg_value", "w_down", "cot", "agg_out",
          "pos", "w_qkv", "w_up")
SEMS = 128


class Names:
    pass


def whole_kernel(*refs):
    mask_ref, ids_ref, query_ref = refs[:3]
    hbm = dict(zip(LOADED, refs[3 : 3 + len(LOADED)]))
    at = 3 + len(LOADED)
    layer_ref, gtok_ref, gqkv_ref, gout_ref, gup_ref, gdown_ref = refs[at : at + 6]
    at += 6
    b = Names()
    for name, ref in zip(SCRATCH, refs[at : at + len(SCRATCH)]):
        setattr(b, name, ref)
    load_sem, ss, rs = refs[at + len(SCRATCH) :]

    v = lax.axis_index("var")
    s = lax.axis_index("space")
    core = lax.rem(s, 2)
    chip = s // 2
    cx, cy = chip // 4, lax.rem(chip, 4)
    sib = s + 1 - 2 * core
    own = pl.ds(pl.multiple_of(v * PART, PART), PART)

    def chip_at(dx, dy):
        return lax.rem(cx + dx, 4) * 4 + lax.rem(cy + dy, 4)

    offsets = [(dx, dy) for dx in range(4) for dy in range(4)]
    around = {o: chip_at(*o) for o in offsets}

    used = [0]
    pending = []

    def fresh(n=1):
        used[0] += n
        assert used[0] <= SEMS
        return used[0] - n

    def wait(sem, ref):
        pltpu.make_async_copy(ref, ref, sem).wait()

    def send(src, dst, k, where):
        pltpu.make_async_remote_copy(
            src_ref=src, dst_ref=dst, send_sem=ss.at[k], recv_sem=rs.at[k],
            device_id=where, device_id_type=MESH,
        ).start()

    def to_core(c):
        return {"space": c}

    def same_core(o):
        return {"space": around[o] * 2 + core}

    loads = {}
    for i, name in enumerate(LOADED):
        loads[name] = pltpu.make_async_copy(hbm[name], getattr(b, name), load_sem.at[i])
        loads[name].start()

    def ready(*names):
        for name in names:
            loads[name].wait()

    barrier = pltpu.get_barrier_semaphore()
    for d in range(1, 8):
        pl.semaphore_signal(barrier, inc=1, device_id={"var": lax.rem(v + d, NV)}, device_id_type=MESH)
    for o in offsets[1:]:
        pl.semaphore_signal(barrier, inc=1, device_id=same_core(o), device_id_type=MESH)
    pl.semaphore_signal(barrier, inc=1, device_id=to_core(sib), device_id_type=MESH)
    for d in range(1, RING):
        pl.semaphore_signal(barrier, inc=1, device_id=to_core(around[0, d] * 2 + 1 - core), device_id_type=MESH)

    def z_scatter(src, land):
        k = fresh()
        for d in FAR_FIRST:
            there = lax.rem(v + d, NV)
            send(src.at[pl.ds(pl.multiple_of(there * PART, PART), PART)], land.at[d - 1], k,
                 {"var": there})
        pending.append((k, land))
        return lambda: wait(rs.at[k], land)

    def z_gather(ref):
        k = fresh()
        for d in FAR_FIRST:
            send(ref.at[own], ref.at[own], k, {"var": lax.rem(v + d, NV)})
        pending.append((k, ref.at[pl.ds(0, 7 * PART)]))
        return lambda: wait(rs.at[k], ref.at[pl.ds(0, 7 * PART)])

    class Halves:
        def __init__(self, src, land, out):
            self.src, self.land, self.out = src, land, out
            self.k = fresh(4)

        def columns(self, half):
            return pl.ds(half * (D // 2), D // 2)

        def start(self, half):
            for d in FAR_FIRST:
                there = lax.rem(v + d, NV)
                send(self.src.at[pl.ds(pl.multiple_of(there * PART, PART), PART), self.columns(half)],
                     self.land.at[half, d - 1], self.k + half, {"var": there})
            pending.append((self.k + half, self.land.at[half]))

        def turn(self, half, add=None):
            wait(rs.at[self.k + half], self.land.at[half])
            parts = [self.src[own, self.columns(half)]] + [self.land[half, d] for d in range(7)]
            if add is None:
                total = parts[0].astype(f32)
                for part in parts[1:]:
                    total = total + part.astype(f32)
            else:
                total = add(parts)
            self.out[own, self.columns(half)] = total.astype(bf16)
            for d in FAR_FIRST:
                send(self.out.at[own, self.columns(half)], self.out.at[own, self.columns(half)],
                     self.k + 2 + half, {"var": lax.rem(v + d, NV)})
            pending.append((self.k + 2 + half, self.land.at[half]))

        def finish(self):
            for half in range(2):
                wait(rs.at[self.k + 2 + half], self.land.at[half])

    def landed(src, land):
        total = src[own].astype(f32)
        for d in range(7):
            total = total + land[d].astype(f32)
        return total

    place = cy * 2 + core
    mates = []
    for d in range(1, RING):
        mates.append((around[0, d] * 2 + core, lax.rem(cy + d, 4) * 2 + core))
        mates.append((around[0, d] * 2 + 1 - core, lax.rem(cy + d, 4) * 2 + 1 - core))
    mates.append((sib, cy * 2 + 1 - core))
    ring = [(same_core((d, 0)), lax.rem(cx + d, 4)) for d in range(1, RING)]

    def team_gather(ref):
        k = fresh()
        for to, _ in mates:
            send(ref.at[place], ref.at[place], k, to_core(to))
        seven = ref.at[pl.ds(0, TEAM - 1)]
        pending.append((k, seven))
        return lambda: wait(rs.at[k], seven)

    def team_scatter(src, land):
        k = fresh()
        for j, (to, t) in enumerate(mates):
            send(src.at[t], land.at[j], k, to_core(to))
        seven = land.at[pl.ds(0, TEAM - 1)]
        pending.append((k, seven))
        return lambda: wait(rs.at[k], seven)

    def ring_gather(ref):
        k = fresh()
        rows = pl.ds(pl.multiple_of(cx * ROWS, ROWS), ROWS)
        for to, _ in ring:
            send(ref.at[rows], ref.at[rows], k, to)
        three = ref.at[pl.ds(0, 3 * ROWS)]
        pending.append((k, three))
        return lambda: wait(rs.at[k], three)

    def ring_scatter(src, land):
        k = fresh()
        for j, (to, t) in enumerate(ring):
            send(src.at[t], land.at[j], k, to)
        pending.append((k, land))
        return lambda: wait(rs.at[k], land)

    class Reduce:
        def __init__(self, name):
            self.part = getattr(b, "wg_part_" + name)
            self.sib = getattr(b, "wg_sib_" + name)
            self.sum = getattr(b, "wg_sum_" + name)
            self.land = getattr(b, "wg_land_" + name)
            self.r = WEIGHT_GRADS[name][0]
            self.k = fresh(2)

        def block(self, which, side):
            return pl.ds(pl.multiple_of((2 * which + side) * self.r, self.r), self.r)

        def start(self):
            for i in range(CHIPS):
                send(self.part.at[self.block(i, 1 - core)], self.sib.at[i], self.k, to_core(sib))
            pending.append((self.k, self.sib))

        def spread(self):
            wait(rs.at[self.k], self.sib)

            def add(i, carry):
                self.sum[i] = (self.part[self.block(i, core)].astype(f32)
                               + self.sib[i].astype(f32)).astype(bf16)
                return carry

            lax.fori_loop(0, CHIPS, add, 0)
            for j, o in enumerate(offsets[1:]):
                send(self.sum.at[around[o]], self.land.at[j], self.k + 1, same_core(o))
            pending.append((self.k + 1, self.land))

        def finish(self):
            wait(rs.at[self.k + 1], self.land)
            total = self.part[self.block(chip, core)].astype(f32) + self.sib[chip].astype(f32)
            for j in range(CHIPS - 1):
                total = total + self.land[j].astype(f32)
            return total

    ready("agg_key")
    row, lane = iota((128, D), 0), iota((128, D), 1)
    spots = (lane // DH == lax.rem(row, H)) & (row < 3 * H)
    spread_one = jnp.where(spots, 1.0, 0.0).astype(bf16)
    rest = jnp.where(spots, query_ref[...], 0.0)
    dirs = jnp.zeros((32, 128), f32)
    for _ in range(3):
        piece = rest.astype(bf16)
        dirs = dirs + nt(b.agg_key[...], piece)
        rest = rest - piece.astype(f32)
    b.dirs_part[...] = dirs.astype(bf16)
    b.dirs_land[0, 0] = dirs.astype(bf16)

    pl.semaphore_wait(barrier, 7 + CHIPS - 1 + 1 + RING - 1)
    dirs_k = fresh(2)
    for j, o in enumerate(offsets[1:]):
        send(b.dirs_part, b.dirs_land.at[0, j + 1], dirs_k, same_core(o))
    pending.append((dirs_k, b.dirs_land.at[0, pl.ds(1, CHIPS - 1)]))

    ready("w_out")
    columns = pl.ds(pl.multiple_of(cx * 256, 256), 256)
    piece = pl.ds(pl.multiple_of(place * PART, PART), PART)
    full_k = fresh(CHIPS + 1)
    for d in FAR_FIRST:
        send(b.w_out.at[piece, columns], b.w_full.at[v, cy, core, :, columns], full_k,
             {"var": lax.rem(v + d, NV)})
    b.w_full[v, cy, core, :, columns] = b.w_out[piece, columns]
    seven = b.w_full.at[pl.ds(0, NV - 1), 0, 0, :, pl.ds(0, 256)]
    eight = b.w_full.at[:, 0, 0, :, pl.ds(0, 256)]
    pending.append((full_k, seven))

    ready("table")
    row, lane = iota((16, V), 0), iota((16, V), 1)
    picks = jnp.zeros((16, V), f32)
    for i in range(SLOTS):
        picks = picks + jnp.where((row == i) & (lane == ids_ref[i]), 1.0, 0.0)
    b.table_rows[...] = nn(picks.astype(bf16), b.table[...])
    ready("pixels", "embed_w")

    def embed(i, carry):
        raw = tn(b.pixels[i], b.embed_w[i])
        b.embedded[pl.ds(pl.multiple_of(i * ROWS, ROWS), ROWS)] = (
            raw + b.table_rows[pl.ds(i, 1)]).astype(bf16)
        return carry

    lax.fori_loop(0, SLOTS, embed, 0)
    wait(rs.at[dirs_k], b.dirs_land.at[0, pl.ds(1, CHIPS - 1)])
    send(b.dirs_land.at[0], b.dirs_land.at[1], dirs_k + 1, to_core(sib))
    pending.append((dirs_k + 1, b.dirs_land.at[1]))
    wait(rs.at[full_k], seven)
    for j, o in enumerate(offsets[1:]):
        send(b.w_full.at[:, cy, core, :, columns], b.w_full.at[:, cy, core, :, columns],
             full_k + 1 + j, same_core(o))
        pending.append((full_k + 1 + j, eight))
    ready("agg_value")

    def value_columns(i, carry):
        columns = pl.ds(pl.multiple_of(i * 256, 256), 256)
        for m in range(2):
            these = pl.ds(m * 768, 768)
            b.values[these, columns] = nn(b.embedded[these], b.agg_value[:, columns])
        return carry

    lax.fori_loop(0, 4, value_columns, 0)
    wait(rs.at[dirs_k + 1], b.dirs_land.at[1])
    for j, o in enumerate(offsets):
        source = lax.rem(cx - o[0] + 4, 4) * 4 + lax.rem(cy - o[1] + 4, 4)
        for side in range(2):
            owner = 2 * source + (core if side == 0 else 1 - core)
            b.dirs[pl.ds(pl.multiple_of(owner * 32, 32), 32)] = b.dirs_land[side, j]

    b.scores[...] = nn(b.embedded[...], b.dirs[...]) * DH ** (-0.5)
    lane = iota((ROWS, 128), 1)
    top = jnp.full((ROWS, 128), MASK_FLOOR, f32)
    for i in range(SLOTS):
        rows = pl.ds(i * ROWS, ROWS)
        top = jnp.maximum(top, jnp.where(mask_ref[i] > 0, b.scores[rows], MASK_FLOOR))
    total = jnp.zeros((ROWS, 128), f32)
    for i in range(SLOTS):
        rows = pl.ds(i * ROWS, ROWS)
        weight = jnp.where(mask_ref[i] > 0, jnp.exp(
            jnp.where(mask_ref[i] > 0, b.scores[rows], MASK_FLOOR) - top), 0.0)
        b.scores[rows] = weight
        total = total + weight
    scale = 1.0 / total
    b.level[...] = top + jnp.log(total)
    for i in range(SLOTS):
        rows = pl.ds(i * ROWS, ROWS)
        b.shares[rows] = thirds(b.scores[rows] * scale, lane)
    level_in = z_scatter(b.level, b.level_land)
    pooled = Halves(b.pooled, b.pooled_land, b.mixed)
    for c in range(4):
        columns = slice(c * 256, (c + 1) * 256)
        wide = nn(b.shares[...], spread_one[:, columns])
        acc = jnp.zeros((ROWS, 256), f32)
        for i in range(SLOTS):
            acc = acc + wide[i * ROWS : (i + 1) * ROWS] * b.values[pl.ds(i * ROWS, ROWS), columns]
        b.pooled[:, columns] = acc.astype(bf16)
        if c % 2:
            pooled.start(c // 2)

    ready("w_down", "cot")
    b.upstream[...] = nt(b.cot[...], b.w_down[...])
    ready("agg_out", "pos")
    level_in()
    levels = [b.level[own]] + [b.level_land[d] for d in range(7)]
    top = functools.reduce(jnp.maximum, levels)
    lifts = [jnp.exp(x - top) for x in levels]
    scale = 1.0 / sum(lifts[1:], lifts[0])
    lane = iota((PART, 128), 1)
    lifts = [nn(thirds(x * scale, lane), spread_one) for x in lifts]
    half = D // 2
    for h in range(2):
        pooled.turn(h, lambda parts: sum(
            lifts[i][:, h * half : (h + 1) * half] * parts[i].astype(f32) for i in range(NV)))
    for j in range(CHIPS - 1):
        wait(rs.at[full_k + 1 + j], eight)
    send(b.w_full.at[:, :, core], b.w_full.at[:, :, core], full_k + CHIPS, to_core(sib))
    pending.append((full_k + CHIPS, b.w_full.at[:, :, 0]))
    ready("w_qkv", "w_up")
    pooled.finish()
    b.tokens[...] = (nn(b.mixed[...], b.agg_out[...]) + b.pos[...].astype(f32)).astype(bf16)

    b.normed_in[...] = layer_norm(b.tokens[...]).astype(bf16)
    mine = pl.ds(pl.multiple_of(cx * ROWS, ROWS), ROWS)
    b.asked[place] = nn(b.normed_in[...], b.w_qkv[0]).astype(bf16) * DH ** (-0.5)
    asked_in = team_gather(b.asked)
    b.keys[mine] = nn(b.normed_in[...], b.w_qkv[1]).astype(bf16)
    keys_in = ring_gather(b.keys)
    b.vals[mine] = nn(b.normed_in[...], b.w_qkv[2]).astype(bf16)
    vals_in = ring_gather(b.vals)

    def chunk(i):
        return pl.ds(pl.multiple_of(i * CHUNK, CHUNK), CHUNK)

    def eights(x):
        return x.reshape(CHUNK // 8, 8, ASKED)

    def stretch(ref, t):
        return jnp.concatenate([ref[t, pl.ds(r, 1), :] for r in range(2 * TEAM)], 1)

    lane = iota((ROWS, 128), 1)
    zero = jnp.zeros((ROWS, 128), bf16)

    def two(ref, block):
        for t in range(TEAM):
            ref[pl.ds(t * ROWS, ROWS)] = jnp.where(lane < DH, block(t), zero)
            ref[pl.ds((TEAM + t) * ROWS, ROWS)] = jnp.where(lane < DH, zero, block(t))

    asked_in()
    two(b.q_two, lambda t: b.asked[t])
    keys_in()
    steps = KEYS // CHUNK

    def score_step(i, top):
        part = nt(b.keys[chunk(i)], b.q_two[...])
        b.probs[chunk(i)] = part
        return jnp.maximum(top, jnp.max(eights(part), 0))

    top = lax.fori_loop(0, steps, score_step, jnp.full((8, ASKED), -jnp.inf, f32))
    top = jnp.max(top, 0, keepdims=True)

    def exp_step(i, total):
        part = jnp.exp(b.probs[chunk(i)] - top)
        b.probs[chunk(i)] = part
        b.probs_b[chunk(i)] = part.astype(bf16)
        return total + jnp.sum(eights(part), 0)

    total = lax.fori_loop(0, steps, exp_step, jnp.zeros((8, ASKED), f32))
    total = jnp.sum(total, 0, keepdims=True)
    span = top + jnp.log(total)
    for r in range(2 * TEAM):
        b.spans[place, pl.ds(r, 1), :] = span[:, r * 128 : (r + 1) * 128]
    spans_in = team_gather(b.spans)
    vals_in()
    scale = 1.0 / total
    for h in range(2):
        side = slice(h * TEAM * ROWS, (h + 1) * TEAM * ROWS)
        part = tn(b.vals[...], b.probs_b[:, side]) * scale[:, side]
        for t in range(TEAM):
            b.shared[t, h * DH : (h + 1) * DH, :] = (
                part[h * DH : (h + 1) * DH, t * ROWS : (t + 1) * ROWS].astype(bf16))
    shared_in = team_scatter(b.shared, b.shared_land)
    spans_in()
    all_spans = b.spans[...]
    top = jnp.max(all_spans, 0)
    whole_span = top + jnp.log(jnp.sum(jnp.exp(all_spans - top[None]), 0))
    shared_in()

    def lift(t):
        rows = [pl.ds(h * TEAM + place, 1) for h in range(2)]
        each = [jnp.exp(b.spans[t, rows[h], :] - b.flat[0, rows[h], :]) for h in range(2)]
        return jnp.where(iota((128, ROWS), 0) < DH, each[0], each[1])

    b.flat[0] = whole_span
    acc = lift(place) * b.shared[place].astype(f32)
    for j, (_, t) in enumerate(mates):
        back = lax.rem(cy + 4 - (j // 2 + 1), 4) * 2 + (core if j % 2 == 0 else 1 - core)
        acc = acc + lift(back if j < 6 else t) * b.shared_land[j].astype(f32)
    b.context[...] = acc.T.astype(bf16)
    b.context_all[v] = b.context[...]

    k = fresh()
    seven = b.context_all.at[pl.ds(0, NV - 1)]
    for d in FAR_FIRST:
        send(b.context_all.at[v], b.context_all.at[v], k, {"var": lax.rem(v + d, NV)})
    pending.append((k, seven))
    factor = jnp.exp(span - stretch(b.flat, 0)) * scale

    def norm_step(i, carry):
        part = b.probs[chunk(i)] * factor
        b.probs[chunk(i)] = part
        b.probs_b[chunk(i)] = part.astype(bf16)
        return carry

    lax.fori_loop(0, steps, norm_step, 0)
    wait(rs.at[full_k + CHIPS], b.w_full.at[:, :, 0])
    wait(rs.at[k], seven)
    all_context = jnp.concatenate([b.context_all[i] for i in range(NV)], 1)
    b.middle[...] = (b.tokens[...].astype(f32)
                     + nn(all_context, b.w_full[...].reshape(D, D))).astype(bf16)

    b.normed_mid[...] = layer_norm(b.middle[...]).astype(bf16)
    pre = nn(b.normed_mid[...], b.w_up[...])
    half = 0.5 * (1.0 + lax.erf(pre * 0.5 ** 0.5))
    b.activated[...] = (pre * half).astype(bf16)
    slope = half + pre * (jnp.exp(-0.5 * pre * pre) * 0.3989422804014327)
    b.grad_pre[...] = (b.upstream[...] * slope).astype(bf16)
    gmid = Halves(b.gmid, b.gmid_land, b.gmid_sum)
    for h in range(2):
        half = pl.ds(h * (D // 2), D // 2)
        b.gmid[:, half] = nt(b.grad_pre[...], b.w_up[half]).astype(bf16)
        gmid.start(h)
    b.down[...] = nn(b.activated[...], b.w_down[...]).astype(bf16)
    wg = {name: Reduce(name) for name in WEIGHT_GRADS}
    wg["down"].part[...] = tn(b.activated[...], b.cot[...]).astype(bf16)
    wg["down"].start()
    gmid.turn(0)
    gmid.turn(1)
    wg["up"].part[...] = tn(b.normed_mid[...], b.grad_pre[...]).astype(bf16)
    wg["up"].start()
    wg["down"].spread()
    gmid.finish()
    b.grad_middle[...] = (b.cot[...].astype(f32) + norm_back(
        b.middle[...], b.gmid_sum[...].astype(f32))).astype(bf16)

    b.graded[place] = nt(b.grad_middle[...], b.w_out[...]).astype(bf16)
    graded_in = team_gather(b.graded)
    down_in = z_scatter(b.down, b.down_land)
    row, lane5 = iota((128, 512), 0), iota((128, 512), 1)
    total = jnp.zeros((512, 256), f32)
    for q in range(4):
        pick = (lane5 // 16 == row // 4) & (lax.rem(lane5, 16) == q * 4 + lax.rem(row, 4))
        picked = nn(b.context[...], jnp.where(pick, 1.0, 0.0).astype(bf16)).astype(bf16)
        total = total + tn(picked, b.grad_middle[:, q * 256 : (q + 1) * 256])
    wg["out"].part[...] = total.astype(bf16)
    graded_in()
    two(b.d_two, lambda t: b.graded[t])

    def delta_step(i, total):
        part = nt(b.vals[chunk(i)], b.d_two[...])
        b.grad_probs[chunk(i)] = part
        return total + jnp.sum(eights(part * b.probs[chunk(i)]), 0)

    delta = lax.fori_loop(0, steps, delta_step, jnp.zeros((8, ASKED), f32))
    delta = jnp.sum(delta, 0, keepdims=True)
    for r in range(2 * TEAM):
        b.deltas[place, pl.ds(r, 1), :] = delta[:, r * 128 : (r + 1) * 128]
    deltas_in = team_gather(b.deltas)
    for t in range(RING):
        b.gv[t] = nn(b.probs_b[pl.ds(t * ROWS, ROWS)], b.d_two[...]).astype(bf16)
    gv_in = ring_scatter(b.gv, b.gv_land)
    deltas_in()
    b.flat[1] = jnp.sum(b.deltas[...], 0)
    delta = stretch(b.flat, 1)

    def back_step(i, carry):
        b.probs_b[chunk(i)] = (b.probs[chunk(i)] * (b.grad_probs[chunk(i)] - delta)).astype(bf16)
        return carry

    lax.fori_loop(0, steps, back_step, 0)
    for h in range(2):
        side = slice(h * TEAM * ROWS, (h + 1) * TEAM * ROWS)
        part = tn(b.keys[...], b.probs_b[:, side])
        for t in range(TEAM):
            b.gq[t, h * DH : (h + 1) * DH, :] = (
                part[h * DH : (h + 1) * DH, t * ROWS : (t + 1) * ROWS].astype(bf16))
    gq_in = team_scatter(b.gq, b.gq_land)
    for t in range(RING):
        b.gk[t] = nn(b.probs_b[pl.ds(t * ROWS, ROWS)], b.q_two[...]).astype(bf16)
    gk_in = ring_scatter(b.gk, b.gk_land)

    down_in()
    b.layer[own] = (b.middle[own].astype(f32) + landed(b.down, b.down_land)).astype(bf16)
    layer_in = z_gather(b.layer)
    wg["out"].start()
    gdown_ref[...] = wg["down"].finish()
    for c, part, land, come in ((2, b.gv, b.gv_land, gv_in), (0, b.gq, b.gq_land, gq_in), (1, b.gk, b.gk_land, gk_in)):
        come()
        total = part[cx if c else place].astype(f32)
        for j in range(RING - 1 if c else TEAM - 1):
            total = total + land[j].astype(f32)
        if c == 0:
            total = total.T * DH ** (-0.5)
        b.grad_rows[:, c * 128 : (c + 1) * 128] = total.astype(bf16)

    gin = Halves(b.gin, b.gin_land, b.gin_sum)
    for h in range(2):
        half = pl.ds(h * (D // 2), D // 2)
        b.gin[:, half] = sum(
            nt(b.grad_rows[:, c * 128 : (c + 1) * 128], b.w_qkv[c, half]) for c in (1, 2, 0)).astype(bf16)
        gin.start(h)
    wg["up"].spread()
    wg["out"].spread()
    wg["qkv"].part[...] = tn(b.normed_in[...], b.grad_rows[...]).astype(bf16)
    wg["qkv"].start()
    wg["qkv"].spread()
    gin.turn(0)
    gin.turn(1)
    gup_ref[...] = wg["up"].finish()
    total = wg["out"].finish()
    for q in range(4):
        gout_ref[:, q * 256 : (q + 1) * 256] = total[q * 4 : (q + 1) * 4]
    total = wg["qkv"].finish()
    for c in range(3):
        gqkv_ref[c] = total[:, c * 128 : (c + 1) * 128]
    gin.finish()
    gtok_ref[...] = (b.grad_middle[...].astype(f32) + norm_back(
        b.tokens[...], b.gin_sum[...].astype(f32))).astype(bf16)
    layer_in()
    layer_ref[...] = b.layer[...]
    for k, ref in pending:
        wait(ss.at[k], ref)


def hand_over(*refs):
    for i in range(6):
        refs[6 + i][...] = refs[i][...]


def shards(pixels, valid_mask, var_ids, embed_weight, var_table, agg_query, agg_key,
           agg_value, agg_out, pos_embed, w_qkv, w_out, w_up, w_down, cotangent):
    in_vmem = pl.BlockSpec(memory_space=pltpu.VMEM)
    in_smem = pl.BlockSpec(memory_space=pltpu.SMEM)
    anywhere = pl.BlockSpec(memory_space=pl.ANY)
    big = (agg_key, w_out, var_table, pixels, embed_weight, agg_value, w_down, cotangent, agg_out,
           pos_embed, w_qkv.transpose(1, 0, 2), w_up)
    shape = jax.ShapeDtypeStruct
    outs = pl.pallas_call(
        whole_kernel,
        out_shape=[shape((ROWS, D), bf16), shape((ROWS, D), bf16), shape((3, 32, 128), f32),
                   shape((4, D), f32), shape((32, HID), f32), shape((16, D), f32)],
        in_specs=[in_smem, in_smem, in_vmem] + [anywhere] * len(big),
        out_specs=[in_vmem] * 6,
        scratch_shapes=[pltpu.VMEM(*spec) for spec in SCRATCH.values()]
        + [pltpu.SemaphoreType.DMA((len(LOADED),)), pltpu.SemaphoreType.DMA((SEMS,)),
           pltpu.SemaphoreType.DMA((SEMS,))],
        compiler_params=pltpu.CompilerParams(
            collective_id=0, has_side_effects=True, vmem_limit_bytes=60 * 2**20),
        name="whole",
    )(valid_mask, var_ids, agg_query.reshape(1, D), *big)
    layer_out, grad_tokens, grad_qkv, grad_out, grad_up, grad_down = pl.pallas_call(
        hand_over,
        out_shape=[shape(x.shape, x.dtype) for x in outs],
        in_specs=[in_vmem] * 6,
        out_specs=[in_vmem] * 6,
        name="hand_over",
    )(*outs)
    return (layer_out, grad_tokens, grad_qkv.transpose(1, 0, 2), grad_out, grad_up, grad_down)


def solution(mesh):
    in_specs = (
        P("var", None, "space"), P("var"), P("var"), P("var", None, None), P(), P(),
        P("space", None), P(), P(), P("space", None), P(None, None, "var"), P("var", None),
        P(None, "var"), P("var", None), P("space", None),
    )
    out_specs = (
        P("space", None), P("space", None), P("space", None, "var"),
        P(("var", "space"), None), P("space", "var"), P(("var", "space"), None),
    )
    return jax.shard_map(shards, mesh=mesh, in_specs=in_specs, out_specs=out_specs, check_vma=False)
```

```python
import functools
import jax
import jax.numpy as jnp
from jax import lax
from jax.experimental import pallas as pl
from jax.experimental.pallas import tpu as pltpu
from jax.sharding import PartitionSpec as P

D = 1024
H = 16
DH = 64
V = 96
NV = 8
CHIPS = 16
SLOTS = V // NV
ROWS = 128
PART = ROWS // NV
HID = 512
RING = 4
TEAM = 8
KEYS = RING * ROWS
ASKED = 2 * TEAM * ROWS
CHUNK = 128
EPSILON = 1e-05
MASK_FLOOR = -1e30
MESH = pl.DeviceIdType.MESH
bf16, f32 = jnp.bfloat16, jnp.float32
FAR_FIRST = (4, 3, 5, 2, 6, 1, 7)


def nn(a, b):
    return jnp.dot(a, b, preferred_element_type=f32)


def nt(a, b):
    return lax.dot_general(a, b, (((1,), (1,)), ((), ())), preferred_element_type=f32)


def tn(a, b):
    return lax.dot_general(a, b, (((0,), (0,)), ((), ())), preferred_element_type=f32)


def mean(values):
    return jnp.mean(values, -1, keepdims=True)


def layer_norm(inputs):
    values = inputs.astype(f32)
    centred = values - mean(values)
    return centred * lax.rsqrt(mean(centred * centred) + EPSILON)


def norm_back(inputs, upstream):
    values = inputs.astype(f32)
    centred = values - mean(values)
    inv_std = lax.rsqrt(mean(centred * centred) + EPSILON)
    normed = centred * inv_std
    return inv_std * (upstream - mean(upstream) - normed * mean(upstream * normed))


def thirds(wide, lane):
    high = wide.astype(bf16).astype(f32)
    rest = wide - high
    middle = rest.astype(bf16).astype(f32)
    low = rest - middle
    picked = jnp.where(lane < H, high, jnp.where(lane < 2 * H, middle, low))
    return jnp.where(lane < 3 * H, picked, 0.0).astype(bf16)


def iota(shape, dim):
    return lax.broadcasted_iota(jnp.int32, shape, dim)


SCRATCH = dict(
    pixels=((SLOTS, 64, ROWS), bf16),
    embed_w=((SLOTS, 64, D), bf16),
    table=((V, D), bf16),
    agg_key=((32, D), bf16),
    agg_value=((D, D), bf16),
    agg_out=((D, D), bf16),
    pos=((ROWS, D), bf16),
    w_qkv=((3, D, 128), bf16),
    w_out=((ROWS, D), bf16),
    w_up=((D, HID), bf16),
    w_down=((HID, D), bf16),
    cot=((ROWS, D), bf16),
    table_rows=((16, D), f32),
    embedded=((SLOTS * ROWS, D), bf16),
    values=((SLOTS * ROWS, D), f32),
    dirs_part=((32, 128), bf16),
    dirs_land=((2, CHIPS, 32, 128), bf16),
    dirs=((D, 128), bf16),
    scores=((SLOTS * ROWS, 128), f32),
    shares=((SLOTS * ROWS, 128), bf16),
    pooled=((ROWS, D), bf16),
    level=((ROWS, 128), f32),
    pooled_land=((2, 7, PART, D // 2), bf16),
    mixed=((ROWS, D), bf16),
    w_full=((NV, RING, 2, PART, D), bf16),
    context_all=((NV, ROWS, 128), bf16),
    level_land=((7, PART, 128), f32),
    tokens=((ROWS, D), bf16),
    normed_in=((ROWS, D), bf16),
    keys=((KEYS, 128), bf16),
    vals=((KEYS, 128), bf16),
    asked=((TEAM, ROWS, 128), bf16),
    q_two=((ASKED, 128), bf16),
    graded=((TEAM, 128, ROWS), bf16),
    d_two=((ASKED, 128), bf16),
    probs=((KEYS, ASKED), f32),
    probs_b=((KEYS, ASKED), bf16),
    low_b=((KEYS, ASKED), bf16),
    part_keep=((TEAM, 128, ROWS), f32),
    low=((TEAM, 128, ROWS), bf16),
    low_land=((TEAM, 128, ROWS), bf16),
    exact=((128, ROWS), f32),
    spans=((TEAM, 2 * TEAM, 128), f32),
    deltas=((TEAM, 8, 128), f32),
    flat=((2, 2 * TEAM, 128), f32),
    shared=((TEAM, 128, ROWS), bf16),
    shared_land=((TEAM, 128, ROWS), bf16),
    context=((ROWS, 128), bf16),
    middle=((ROWS, D), bf16),
    normed_mid=((ROWS, D), bf16),
    upstream=((ROWS, HID), f32),
    activated=((ROWS, HID), bf16),
    grad_pre=((ROWS, HID), bf16),
    gmid=((ROWS, D), bf16),
    gmid_land=((2, 7, PART, D // 2), bf16),
    gmid_sum=((ROWS, D), bf16),
    down=((ROWS, D), bf16),
    down_land=((7, PART, D), bf16),
    layer=((ROWS, D), bf16),
    grad_middle=((ROWS, D), bf16),
    gq=((TEAM, 128, ROWS), bf16),
    gq_land=((TEAM - 1, 128, ROWS), bf16),
    gk=((RING, ROWS, 128), bf16),
    gv=((RING, ROWS, 128), bf16),
    gk_land=((RING - 1, ROWS, 128), bf16),
    gv_land=((RING - 1, ROWS, 128), bf16),
    grad_rows=((ROWS, 384), bf16),
    gin=((ROWS, D), bf16),
    gin_land=((2, 7, PART, D // 2), bf16),
    gin_sum=((ROWS, D), bf16),
)
WEIGHT_GRADS = dict(down=(16, D), up=(32, HID), out=(16, 256), qkv=(32, 384))
for _name, (_r, _w) in WEIGHT_GRADS.items():
    SCRATCH["wg_part_" + _name] = ((32 * _r, _w), bf16)
    SCRATCH["wg_sib_" + _name] = ((CHIPS, _r, _w), bf16)
    SCRATCH["wg_sum_" + _name] = ((CHIPS, _r, _w), bf16)
    SCRATCH["wg_land_" + _name] = ((CHIPS - 1, _r, _w), bf16)
LOADED = ("agg_key", "table", "pixels", "embed_w", "w_out", "agg_value", "w_down", "cot", "agg_out",
          "pos", "w_qkv", "w_up")
EARLY = 4
SEMS = 128


class Names:
    pass


def whole_kernel(*refs):
    mask_ref, ids_ref, query_ref = refs[:3]
    hbm = dict(zip(LOADED, refs[3 : 3 + len(LOADED)]))
    at = 3 + len(LOADED)
    layer_ref, gtok_ref, gqkv_ref, gout_ref, gup_ref, gdown_ref = refs[at : at + 6]
    at += 6
    b = Names()
    for name, ref in zip(SCRATCH, refs[at : at + len(SCRATCH)]):
        setattr(b, name, ref)
    load_sem, ss, rs = refs[at + len(SCRATCH) :]

    v = lax.axis_index("var")
    s = lax.axis_index("space")
    core = lax.rem(s, 2)
    chip = s // 2
    cx, cy = chip // 4, lax.rem(chip, 4)
    sib = s + 1 - 2 * core
    own = pl.ds(pl.multiple_of(v * PART, PART), PART)

    def chip_at(dx, dy):
        return lax.rem(cx + dx, 4) * 4 + lax.rem(cy + dy, 4)

    offsets = [(dx, dy) for dx in range(4) for dy in range(4)]
    around = {o: chip_at(*o) for o in offsets}

    used = [0]
    pending = []

    def fresh(n=1):
        used[0] += n
        assert used[0] <= SEMS
        return used[0] - n

    def wait(sem, ref):
        pltpu.make_async_copy(ref, ref, sem).wait()

    def send(src, dst, k, where):
        pltpu.make_async_remote_copy(
            src_ref=src, dst_ref=dst, send_sem=ss.at[k], recv_sem=rs.at[k],
            device_id=where, device_id_type=MESH,
        ).start()

    def to_core(c):
        return {"space": c}

    def same_core(o):
        return {"space": around[o] * 2 + core}

    loads = {}
    for i, name in enumerate(LOADED):
        loads[name] = pltpu.make_async_copy(hbm[name], getattr(b, name), load_sem.at[i])
        if i < EARLY:
            loads[name].start()

    def ready(*names):
        for name in names:
            loads[name].wait()

    barrier = pltpu.get_barrier_semaphore()
    for d in range(1, 8):
        pl.semaphore_signal(barrier, inc=1, device_id={"var": lax.rem(v + d, NV)}, device_id_type=MESH)
    for o in offsets[1:]:
        pl.semaphore_signal(barrier, inc=1, device_id=same_core(o), device_id_type=MESH)
    pl.semaphore_signal(barrier, inc=1, device_id=to_core(sib), device_id_type=MESH)
    for d in range(1, RING):
        pl.semaphore_signal(barrier, inc=1, device_id=to_core(around[0, d] * 2 + 1 - core), device_id_type=MESH)

    def z_scatter(src, land):
        k = fresh()
        for d in FAR_FIRST:
            there = lax.rem(v + d, NV)
            send(src.at[pl.ds(pl.multiple_of(there * PART, PART), PART)], land.at[d - 1], k,
                 {"var": there})
        pending.append((k, land))
        return lambda: wait(rs.at[k], land)

    def z_gather(ref):
        k = fresh()
        for d in FAR_FIRST:
            send(ref.at[own], ref.at[own], k, {"var": lax.rem(v + d, NV)})
        pending.append((k, ref.at[pl.ds(0, 7 * PART)]))
        return lambda: wait(rs.at[k], ref.at[pl.ds(0, 7 * PART)])

    class Halves:
        def __init__(self, src, land, out):
            self.src, self.land, self.out = src, land, out
            self.k = fresh(4)

        def columns(self, half):
            return pl.ds(half * (D // 2), D // 2)

        def start(self, half):
            for d in FAR_FIRST:
                there = lax.rem(v + d, NV)
                send(self.src.at[pl.ds(pl.multiple_of(there * PART, PART), PART), self.columns(half)],
                     self.land.at[half, d - 1], self.k + half, {"var": there})
            pending.append((self.k + half, self.land.at[half]))

        def turn(self, half, add=None):
            wait(rs.at[self.k + half], self.land.at[half])
            parts = [self.src[own, self.columns(half)]] + [self.land[half, d] for d in range(7)]
            if add is None:
                total = parts[0].astype(f32)
                for part in parts[1:]:
                    total = total + part.astype(f32)
            else:
                total = add(parts)
            self.out[own, self.columns(half)] = total.astype(bf16)
            for d in FAR_FIRST:
                send(self.out.at[own, self.columns(half)], self.out.at[own, self.columns(half)],
                     self.k + 2 + half, {"var": lax.rem(v + d, NV)})
            pending.append((self.k + 2 + half, self.land.at[half]))

        def finish(self):
            for half in range(2):
                wait(rs.at[self.k + 2 + half], self.land.at[half])

    def landed(src, land):
        total = src[own].astype(f32)
        for d in range(7):
            total = total + land[d].astype(f32)
        return total

    place = cy * 2 + core
    mates = []
    for d in range(1, RING):
        mates.append((around[0, d] * 2 + core, lax.rem(cy + d, 4) * 2 + core))
        mates.append((around[0, d] * 2 + 1 - core, lax.rem(cy + d, 4) * 2 + 1 - core))
    mates.append((sib, cy * 2 + 1 - core))
    ring = [(same_core((d, 0)), lax.rem(cx + d, 4)) for d in range(1, RING)]

    def team_gather(ref):
        k = fresh()
        for to, _ in mates:
            send(ref.at[place], ref.at[place], k, to_core(to))
        seven = ref.at[pl.ds(0, TEAM - 1)]
        pending.append((k, seven))
        return lambda: wait(rs.at[k], seven)

    def team_scatter(src, land):
        k = fresh()
        for j, (to, t) in enumerate(mates):
            send(src.at[t], land.at[j], k, to_core(to))
        seven = land.at[pl.ds(0, TEAM - 1)]
        pending.append((k, seven))
        return lambda: wait(rs.at[k], seven)

    def ring_gather(ref):
        k = fresh()
        rows = pl.ds(pl.multiple_of(cx * ROWS, ROWS), ROWS)
        for to, _ in ring:
            send(ref.at[rows], ref.at[rows], k, to)
        three = ref.at[pl.ds(0, 3 * ROWS)]
        pending.append((k, three))
        return lambda: wait(rs.at[k], three)

    def ring_scatter(src, land):
        k = fresh()
        for j, (to, t) in enumerate(ring):
            send(src.at[t], land.at[j], k, to)
        pending.append((k, land))
        return lambda: wait(rs.at[k], land)

    class Reduce:
        def __init__(self, name):
            self.part = getattr(b, "wg_part_" + name)
            self.sib = getattr(b, "wg_sib_" + name)
            self.sum = getattr(b, "wg_sum_" + name)
            self.land = getattr(b, "wg_land_" + name)
            self.r = WEIGHT_GRADS[name][0]
            self.k = fresh(2)

        def block(self, which, side):
            return pl.ds(pl.multiple_of((2 * which + side) * self.r, self.r), self.r)

        def start(self):
            for i in range(CHIPS):
                send(self.part.at[self.block(i, 1 - core)], self.sib.at[i], self.k, to_core(sib))
            pending.append((self.k, self.sib))

        def spread(self):
            wait(rs.at[self.k], self.sib)

            def add(i, carry):
                self.sum[i] = (self.part[self.block(i, core)].astype(f32)
                               + self.sib[i].astype(f32)).astype(bf16)
                return carry

            lax.fori_loop(0, CHIPS, add, 0)
            for j, o in enumerate(offsets[1:]):
                send(self.sum.at[around[o]], self.land.at[j], self.k + 1, same_core(o))
            pending.append((self.k + 1, self.land))

        def finish(self):
            wait(rs.at[self.k + 1], self.land)
            total = self.part[self.block(chip, core)].astype(f32) + self.sib[chip].astype(f32)
            for j in range(CHIPS - 1):
                total = total + self.land[j].astype(f32)
            return total

    ready("agg_key")
    row, lane = iota((128, D), 0), iota((128, D), 1)
    spots = (lane // DH == lax.rem(row, H)) & (row < 3 * H)
    spread_one = jnp.where(spots, 1.0, 0.0).astype(bf16)
    rest = jnp.where(spots, query_ref[...], 0.0)
    dirs = jnp.zeros((32, 128), f32)
    for _ in range(3):
        piece = rest.astype(bf16)
        dirs = dirs + nt(b.agg_key[...], piece)
        rest = rest - piece.astype(f32)
    b.dirs_part[...] = dirs.astype(bf16)
    b.dirs_land[0, 0] = dirs.astype(bf16)

    ready("table")
    row, lane = iota((16, V), 0), iota((16, V), 1)
    picks = jnp.zeros((16, V), f32)
    for i in range(SLOTS):
        picks = picks + jnp.where((row == i) & (lane == ids_ref[i]), 1.0, 0.0)
    b.table_rows[...] = nn(picks.astype(bf16), b.table[...])
    ready("pixels", "embed_w")
    for name in LOADED[EARLY:]:
        loads[name].start()

    def embed(i, carry):
        raw = tn(b.pixels[i], b.embed_w[i])
        b.embedded[pl.ds(pl.multiple_of(i * ROWS, ROWS), ROWS)] = (
            raw + b.table_rows[pl.ds(i, 1)]).astype(bf16)
        return carry

    lax.fori_loop(0, SLOTS, embed, 0, unroll=3)
    pl.semaphore_wait(barrier, 7 + CHIPS - 1 + 1 + RING - 1)
    dirs_k = fresh(2)
    for j, o in enumerate(offsets[1:]):
        send(b.dirs_part, b.dirs_land.at[0, j + 1], dirs_k, same_core(o))
    pending.append((dirs_k, b.dirs_land.at[0, pl.ds(1, CHIPS - 1)]))

    ready("w_out")
    columns = pl.ds(pl.multiple_of(cx * 256, 256), 256)
    piece = pl.ds(pl.multiple_of(place * PART, PART), PART)
    full_k = fresh(CHIPS + 1)
    for d in FAR_FIRST:
        send(b.w_out.at[piece, columns], b.w_full.at[v, cy, core, :, columns], full_k,
             {"var": lax.rem(v + d, NV)})
    b.w_full[v, cy, core, :, columns] = b.w_out[piece, columns]
    seven = b.w_full.at[pl.ds(0, NV - 1), 0, 0, :, pl.ds(0, 256)]
    eight = b.w_full.at[:, 0, 0, :, pl.ds(0, 256)]
    pending.append((full_k, seven))


    ready("agg_value")

    def value_columns(i, carry):
        columns = pl.ds(pl.multiple_of(i * 256, 256), 256)
        for m in range(2):
            these = pl.ds(m * 768, 768)
            b.values[these, columns] = nn(b.embedded[these], b.agg_value[:, columns])
        return carry

    lax.fori_loop(0, 3, value_columns, 0)
    wait(rs.at[dirs_k], b.dirs_land.at[0, pl.ds(1, CHIPS - 1)])
    send(b.dirs_land.at[0], b.dirs_land.at[1], dirs_k + 1, to_core(sib))
    pending.append((dirs_k + 1, b.dirs_land.at[1]))
    wait(rs.at[full_k], seven)
    for j, o in enumerate(offsets[1:]):
        send(b.w_full.at[:, cy, core, :, columns], b.w_full.at[:, cy, core, :, columns],
             full_k + 1 + j, same_core(o))
        pending.append((full_k + 1 + j, eight))
    value_columns(3, 0)
    wait(rs.at[dirs_k + 1], b.dirs_land.at[1])
    for j, o in enumerate(offsets):
        source = lax.rem(cx - o[0] + 4, 4) * 4 + lax.rem(cy - o[1] + 4, 4)
        for side in range(2):
            owner = 2 * source + (core if side == 0 else 1 - core)
            b.dirs[pl.ds(pl.multiple_of(owner * 32, 32), 32)] = b.dirs_land[side, j]

    b.scores[...] = nn(b.embedded[...], b.dirs[...]) * DH ** (-0.5)
    lane = iota((ROWS, 128), 1)
    top = jnp.full((ROWS, 128), MASK_FLOOR, f32)
    for i in range(SLOTS):
        rows = pl.ds(i * ROWS, ROWS)
        top = jnp.maximum(top, jnp.where(mask_ref[i] > 0, b.scores[rows], MASK_FLOOR))
    total = jnp.zeros((ROWS, 128), f32)
    for i in range(SLOTS):
        rows = pl.ds(i * ROWS, ROWS)
        weight = jnp.where(mask_ref[i] > 0, jnp.exp(
            jnp.where(mask_ref[i] > 0, b.scores[rows], MASK_FLOOR) - top), 0.0)
        b.scores[rows] = weight
        total = total + weight
    scale = 1.0 / total
    b.level[...] = top + jnp.log(total)
    for i in range(SLOTS):
        rows = pl.ds(i * ROWS, ROWS)
        b.shares[rows] = thirds(b.scores[rows] * scale, lane)
    level_in = z_scatter(b.level, b.level_land)
    pooled = Halves(b.pooled, b.pooled_land, b.mixed)
    for c in range(4):
        columns = slice(c * 256, (c + 1) * 256)
        wide = nn(b.shares[...], spread_one[:, columns])
        acc = jnp.zeros((ROWS, 256), f32)
        for i in range(SLOTS):
            acc = acc + wide[i * ROWS : (i + 1) * ROWS] * b.values[pl.ds(i * ROWS, ROWS), columns]
        b.pooled[:, columns] = acc.astype(bf16)
        if c % 2:
            pooled.start(c // 2)

    ready("w_down", "cot")
    b.upstream[...] = nt(b.cot[...], b.w_down[...])
    ready("agg_out", "pos")
    level_in()
    levels = [b.level[own]] + [b.level_land[d] for d in range(7)]
    top = functools.reduce(jnp.maximum, levels)
    lifts = [jnp.exp(x - top) for x in levels]
    scale = 1.0 / sum(lifts[1:], lifts[0])
    lane = iota((PART, 128), 1)
    lifts = [nn(thirds(x * scale, lane), spread_one) for x in lifts]
    half = D // 2
    for h in range(2):
        pooled.turn(h, lambda parts: sum(
            lifts[i][:, h * half : (h + 1) * half] * parts[i].astype(f32) for i in range(NV)))
    for j in range(CHIPS - 1):
        wait(rs.at[full_k + 1 + j], eight)
    send(b.w_full.at[:, :, core], b.w_full.at[:, :, core], full_k + CHIPS, to_core(sib))
    pending.append((full_k + CHIPS, b.w_full.at[:, :, 0]))
    ready("w_qkv", "w_up")
    pooled.finish()
    b.tokens[...] = (nn(b.mixed[...], b.agg_out[...]) + b.pos[...].astype(f32)).astype(bf16)

    b.normed_in[...] = layer_norm(b.tokens[...]).astype(bf16)
    mine = pl.ds(pl.multiple_of(cx * ROWS, ROWS), ROWS)
    b.asked[place] = nn(b.normed_in[...], b.w_qkv[0]).astype(bf16) * DH ** (-0.5)
    asked_in = team_gather(b.asked)
    b.keys[mine] = nn(b.normed_in[...], b.w_qkv[1]).astype(bf16)
    keys_in = ring_gather(b.keys)
    b.vals[mine] = nn(b.normed_in[...], b.w_qkv[2]).astype(bf16)
    vals_in = ring_gather(b.vals)

    def chunk(i):
        return pl.ds(pl.multiple_of(i * CHUNK, CHUNK), CHUNK)

    def eights(x):
        return x.reshape(CHUNK // 8, 8, ASKED)

    def stretch(ref, t):
        return jnp.concatenate([ref[t, pl.ds(r, 1), :] for r in range(2 * TEAM)], 1)

    lane = iota((ROWS, 128), 1)
    zero = jnp.zeros((ROWS, 128), bf16)

    def two(ref, block):
        for t in range(TEAM):
            ref[pl.ds(t * ROWS, ROWS)] = jnp.where(lane < DH, block(t), zero)
            ref[pl.ds((TEAM + t) * ROWS, ROWS)] = jnp.where(lane < DH, zero, block(t))

    asked_in()
    two(b.q_two, lambda t: b.asked[t])
    keys_in()
    steps = KEYS // CHUNK

    def score_step(i, top):
        part = nt(b.keys[chunk(i)], b.q_two[...])
        b.probs[chunk(i)] = part
        return jnp.maximum(top, jnp.max(eights(part), 0))

    top = lax.fori_loop(0, steps, score_step, jnp.full((8, ASKED), -jnp.inf, f32))
    top = jnp.max(top, 0, keepdims=True)

    def exp_step(i, total):
        part = jnp.exp(b.probs[chunk(i)] - top)
        b.probs[chunk(i)] = part
        b.probs_b[chunk(i)] = part.astype(bf16)
        return total + jnp.sum(eights(part), 0)

    total = lax.fori_loop(0, steps, exp_step, jnp.zeros((8, ASKED), f32))
    total = jnp.sum(total, 0, keepdims=True)
    span = top + jnp.log(total)
    for r in range(2 * TEAM):
        b.spans[place, pl.ds(r, 1), :] = span[:, r * 128 : (r + 1) * 128]
    spans_in = team_gather(b.spans)
    vals_in()
    scale = 1.0 / total
    for h in range(2):
        side = slice(h * TEAM * ROWS, (h + 1) * TEAM * ROWS)
        part = tn(b.vals[...], b.probs_b[:, side]) * scale[:, side]
        for t in range(TEAM):
            here = part[h * DH : (h + 1) * DH, t * ROWS : (t + 1) * ROWS]
            b.part_keep[t, h * DH : (h + 1) * DH, :] = here
            b.shared[t, h * DH : (h + 1) * DH, :] = here.astype(bf16)
    shared_in = team_scatter(b.shared, b.shared_land)

    def low_step(i, carry):
        b.low_b[chunk(i)] = (b.probs[chunk(i)] - b.probs_b[chunk(i)].astype(f32)).astype(bf16)
        return carry

    lax.fori_loop(0, steps, low_step, 0)
    for h in range(2):
        side = slice(h * TEAM * ROWS, (h + 1) * TEAM * ROWS)
        part = tn(b.vals[...], b.low_b[:, side]) * scale[:, side]
        rows = slice(h * DH, (h + 1) * DH)
        for t in range(TEAM):
            b.low[t, rows, :] = (part[rows, t * ROWS : (t + 1) * ROWS] + (
                b.part_keep[t, rows, :] - b.shared[t, rows, :].astype(f32))).astype(bf16)
    low_in = team_scatter(b.low, b.low_land)
    spans_in()
    all_spans = b.spans[...]
    top = jnp.max(all_spans, 0)
    whole_span = top + jnp.log(jnp.sum(jnp.exp(all_spans - top[None]), 0))
    shared_in()

    def lift(t):
        rows = [pl.ds(h * TEAM + place, 1) for h in range(2)]
        each = [jnp.exp(b.spans[t, rows[h], :] - b.flat[0, rows[h], :]) for h in range(2)]
        return jnp.where(iota((128, ROWS), 0) < DH, each[0], each[1])

    b.flat[0] = whole_span
    lifted = [lift(place)]
    acc = lifted[0] * b.shared[place].astype(f32)
    for j, (_, t) in enumerate(mates):
        back = lax.rem(cy + 4 - (j // 2 + 1), 4) * 2 + (core if j % 2 == 0 else 1 - core)
        lifted.append(lift(back if j < 6 else t))
        acc = acc + lifted[-1] * b.shared_land[j].astype(f32)
    b.context[...] = acc.T.astype(bf16)
    b.context_all[v] = b.context[...]

    k = fresh()
    seven = b.context_all.at[pl.ds(0, NV - 1)]
    for d in FAR_FIRST:
        send(b.context_all.at[v], b.context_all.at[v], k, {"var": lax.rem(v + d, NV)})
    pending.append((k, seven))
    factor = jnp.exp(span - stretch(b.flat, 0)) * scale

    def norm_step(i, carry):
        part = b.probs[chunk(i)] * factor
        b.probs[chunk(i)] = part
        b.probs_b[chunk(i)] = part.astype(bf16)
        return carry

    lax.fori_loop(0, steps, norm_step, 0)
    low_in()
    acc = acc + lifted[0] * b.low[place].astype(f32)
    for j in range(TEAM - 1):
        acc = acc + lifted[j + 1] * b.low_land[j].astype(f32)
    b.exact[...] = acc
    wait(rs.at[full_k + CHIPS], b.w_full.at[:, :, 0])
    wait(rs.at[k], seven)
    all_context = jnp.concatenate([b.context_all[i] for i in range(NV)], 1)
    b.middle[...] = (b.tokens[...].astype(f32)
                     + nn(all_context, b.w_full[...].reshape(D, D))).astype(bf16)

    b.normed_mid[...] = layer_norm(b.middle[...]).astype(bf16)
    pre = nn(b.normed_mid[...], b.w_up[...])
    half = 0.5 * (1.0 + lax.erf(pre * 0.5 ** 0.5))
    b.activated[...] = (pre * half).astype(bf16)
    slope = half + pre * (jnp.exp(-0.5 * pre * pre) * 0.3989422804014327)
    b.grad_pre[...] = (b.upstream[...] * slope).astype(bf16)
    gmid = Halves(b.gmid, b.gmid_land, b.gmid_sum)
    for h in range(2):
        half = pl.ds(h * (D // 2), D // 2)
        b.gmid[:, half] = nt(b.grad_pre[...], b.w_up[half]).astype(bf16)
        gmid.start(h)
    b.down[...] = nn(b.activated[...], b.w_down[...]).astype(bf16)
    wg = {name: Reduce(name) for name in WEIGHT_GRADS}
    wg["down"].part[...] = tn(b.activated[...], b.cot[...]).astype(bf16)
    wg["down"].start()
    gmid.turn(0)
    gmid.turn(1)
    wg["up"].part[...] = tn(b.normed_mid[...], b.grad_pre[...]).astype(bf16)
    wg["up"].start()
    wg["down"].spread()
    gmid.finish()
    b.grad_middle[...] = (b.cot[...].astype(f32) + norm_back(
        b.middle[...], b.gmid_sum[...].astype(f32))).astype(bf16)

    b.graded[place] = nt(b.grad_middle[...], b.w_out[...]).astype(bf16)
    graded_in = team_gather(b.graded)
    products = b.graded[place].astype(f32).T * b.exact[...]
    b.deltas[place] = jnp.zeros((8, 128), f32)
    for h in range(2):
        b.deltas[place, pl.ds(h, 1), :] = jnp.sum(products[h * DH : (h + 1) * DH], 0, keepdims=True)
    deltas_in = team_gather(b.deltas)
    down_in = z_scatter(b.down, b.down_land)
    row, lane5 = iota((128, 512), 0), iota((128, 512), 1)
    total = jnp.zeros((512, 256), f32)
    for q in range(4):
        pick = (lane5 // 16 == row // 4) & (lax.rem(lane5, 16) == q * 4 + lax.rem(row, 4))
        picked = nn(b.context[...], jnp.where(pick, 1.0, 0.0).astype(bf16)).astype(bf16)
        total = total + tn(picked, b.grad_middle[:, q * 256 : (q + 1) * 256])
    wg["out"].part[...] = total.astype(bf16)
    wg["out"].start()
    graded_in()
    two(b.d_two, lambda t: b.graded[t])

    for t in range(RING):
        b.gv[t] = nn(b.probs_b[pl.ds(t * ROWS, ROWS)], b.d_two[...]).astype(bf16)
    gv_in = ring_scatter(b.gv, b.gv_land)
    deltas_in()
    delta = jnp.concatenate(
        [b.deltas[t, pl.ds(h, 1), :] for h in range(2) for t in range(TEAM)], 1)

    def back_step(i, carry):
        part = nt(b.vals[chunk(i)], b.d_two[...])
        b.probs_b[chunk(i)] = (b.probs[chunk(i)] * (part - delta)).astype(bf16)
        return carry

    lax.fori_loop(0, steps, back_step, 0)
    for h in range(2):
        side = slice(h * TEAM * ROWS, (h + 1) * TEAM * ROWS)
        part = tn(b.keys[...], b.probs_b[:, side])
        for t in range(TEAM):
            b.gq[t, h * DH : (h + 1) * DH, :] = (
                part[h * DH : (h + 1) * DH, t * ROWS : (t + 1) * ROWS].astype(bf16))
    gq_in = team_scatter(b.gq, b.gq_land)
    for t in range(RING):
        b.gk[t] = nn(b.probs_b[pl.ds(t * ROWS, ROWS)], b.q_two[...]).astype(bf16)
    gk_in = ring_scatter(b.gk, b.gk_land)

    down_in()
    b.layer[own] = (b.middle[own].astype(f32) + landed(b.down, b.down_land)).astype(bf16)
    layer_in = z_gather(b.layer)
    wg["up"].spread()
    wg["out"].spread()
    for c, part, land, come in ((2, b.gv, b.gv_land, gv_in), (0, b.gq, b.gq_land, gq_in), (1, b.gk, b.gk_land, gk_in)):
        come()
        total = part[cx if c else place].astype(f32)
        for j in range(RING - 1 if c else TEAM - 1):
            total = total + land[j].astype(f32)
        if c == 0:
            total = total.T * DH ** (-0.5)
        b.grad_rows[:, c * 128 : (c + 1) * 128] = total.astype(bf16)

    gin = Halves(b.gin, b.gin_land, b.gin_sum)
    for h in range(2):
        half = pl.ds(h * (D // 2), D // 2)
        b.gin[:, half] = sum(
            nt(b.grad_rows[:, c * 128 : (c + 1) * 128], b.w_qkv[c, half]) for c in (1, 2, 0)).astype(bf16)
        gin.start(h)
    wg["qkv"].part[...] = tn(b.normed_in[...], b.grad_rows[...]).astype(bf16)
    wg["qkv"].start()
    gdown_ref[...] = wg["down"].finish()
    wg["qkv"].spread()
    gin.turn(0)
    gin.turn(1)
    gup_ref[...] = wg["up"].finish()
    total = wg["out"].finish()
    for q in range(4):
        gout_ref[:, q * 256 : (q + 1) * 256] = total[q * 4 : (q + 1) * 4]
    total = wg["qkv"].finish()
    for c in range(3):
        gqkv_ref[c] = total[:, c * 128 : (c + 1) * 128]
    gin.finish()
    gtok_ref[...] = (b.grad_middle[...].astype(f32) + norm_back(
        b.tokens[...], b.gin_sum[...].astype(f32))).astype(bf16)
    layer_in()
    layer_ref[...] = b.layer[...]
    for k, ref in pending:
        wait(ss.at[k], ref)


def hand_over(*refs):
    for i in range(6):
        refs[6 + i][...] = refs[i][...]


def shards(pixels, valid_mask, var_ids, embed_weight, var_table, agg_query, agg_key,
           agg_value, agg_out, pos_embed, w_qkv, w_out, w_up, w_down, cotangent):
    in_vmem = pl.BlockSpec(memory_space=pltpu.VMEM)
    in_smem = pl.BlockSpec(memory_space=pltpu.SMEM)
    anywhere = pl.BlockSpec(memory_space=pl.ANY)
    big = (agg_key, var_table, pixels, embed_weight, w_out, agg_value, w_down, cotangent, agg_out,
           pos_embed, w_qkv.transpose(1, 0, 2), w_up)
    shape = jax.ShapeDtypeStruct
    outs = pl.pallas_call(
        whole_kernel,
        out_shape=[shape((ROWS, D), bf16), shape((ROWS, D), bf16), shape((3, 32, 128), f32),
                   shape((4, D), f32), shape((32, HID), f32), shape((16, D), f32)],
        in_specs=[in_smem, in_smem, in_vmem] + [anywhere] * len(big),
        out_specs=[in_vmem] * 6,
        scratch_shapes=[pltpu.VMEM(*spec) for spec in SCRATCH.values()]
        + [pltpu.SemaphoreType.DMA((len(LOADED),)), pltpu.SemaphoreType.DMA((SEMS,)),
           pltpu.SemaphoreType.DMA((SEMS,))],
        compiler_params=pltpu.CompilerParams(
            collective_id=0, has_side_effects=True, vmem_limit_bytes=60 * 2**20),
        name="whole",
    )(valid_mask, var_ids, agg_query.reshape(1, D), *big)
    layer_out, grad_tokens, grad_qkv, grad_out, grad_up, grad_down = pl.pallas_call(
        hand_over,
        out_shape=[shape(x.shape, x.dtype) for x in outs],
        in_specs=[in_vmem] * 6,
        out_specs=[in_vmem] * 6,
        name="hand_over",
    )(*outs)
    return (layer_out, grad_tokens, grad_qkv.transpose(1, 0, 2), grad_out, grad_up, grad_down)


def solution(mesh):
    in_specs = (
        P("var", None, "space"), P("var"), P("var"), P("var", None, None), P(), P(),
        P("space", None), P(), P(), P("space", None), P(None, None, "var"), P("var", None),
        P(None, "var"), P("var", None), P("space", None),
    )
    out_specs = (
        P("space", None), P("space", None), P("space", None, "var"),
        P(("var", "space"), None), P("space", "var"), P(("var", "space"), None),
    )
    return jax.shard_map(shards, mesh=mesh, in_specs=in_specs, out_specs=out_specs, check_vma=False)
```

```python
import functools
import jax
import jax.numpy as jnp
from jax import lax
from jax.experimental import pallas as pl
from jax.experimental.pallas import tpu as pltpu
from jax.sharding import PartitionSpec as P

D = 1024
H = 16
DH = 64
V = 96
NV = 8
CHIPS = 16
SLOTS = V // NV
ROWS = 128
PART = ROWS // NV
HID = 512
RING = 4
TEAM = 8
KEYS = RING * ROWS
ASKED = 2 * TEAM * ROWS
CHUNK = 128
EPSILON = 1e-05
MASK_FLOOR = -1e30
MESH = pl.DeviceIdType.MESH
bf16, f32 = jnp.bfloat16, jnp.float32
FAR_FIRST = (4, 3, 5, 2, 6, 1, 7)


def nn(a, b):
    return jnp.dot(a, b, preferred_element_type=f32)


def nt(a, b):
    return lax.dot_general(a, b, (((1,), (1,)), ((), ())), preferred_element_type=f32)


def tn(a, b):
    return lax.dot_general(a, b, (((0,), (0,)), ((), ())), preferred_element_type=f32)


def mean(values):
    return jnp.mean(values, -1, keepdims=True)


def layer_norm(inputs):
    values = inputs.astype(f32)
    centred = values - mean(values)
    return centred * lax.rsqrt(mean(centred * centred) + EPSILON)


def norm_back(inputs, upstream):
    values = inputs.astype(f32)
    centred = values - mean(values)
    inv_std = lax.rsqrt(mean(centred * centred) + EPSILON)
    normed = centred * inv_std
    return inv_std * (upstream - mean(upstream) - normed * mean(upstream * normed))


def thirds(wide, lane):
    high = wide.astype(bf16).astype(f32)
    rest = wide - high
    middle = rest.astype(bf16).astype(f32)
    low = rest - middle
    picked = jnp.where(lane < H, high, jnp.where(lane < 2 * H, middle, low))
    return jnp.where(lane < 3 * H, picked, 0.0).astype(bf16)


def iota(shape, dim):
    return lax.broadcasted_iota(jnp.int32, shape, dim)


SCRATCH = dict(
    pixels=((SLOTS, 64, ROWS), bf16),
    embed_w=((SLOTS, 64, D), bf16),
    table=((V, D), bf16),
    agg_key=((32, D), bf16),
    agg_value=((D, D), bf16),
    agg_out=((D, D), bf16),
    pos=((ROWS, D), bf16),
    w_qkv=((3, D, 128), bf16),
    w_out=((ROWS, D), bf16),
    w_up=((D, HID), bf16),
    w_down=((HID, D), bf16),
    cot=((ROWS, D), bf16),
    table_rows=((16, D), f32),
    embedded=((SLOTS * ROWS, D), bf16),
    values=((SLOTS * ROWS, D), f32),
    dirs_part=((32, 128), bf16),
    dirs_land=((2, CHIPS, 32, 128), bf16),
    dirs=((D, 128), bf16),
    scores=((SLOTS * ROWS, 128), f32),
    shares=((SLOTS * ROWS, 128), bf16),
    pooled=((ROWS, D), bf16),
    level=((ROWS, 128), f32),
    pooled_land=((2, 7, PART, D // 2), bf16),
    mixed=((ROWS, D), bf16),
    w_full=((NV, RING, 2, PART, D), bf16),
    context_all=((NV, ROWS, 128), bf16),
    level_land=((7, PART, 128), f32),
    tokens=((ROWS, D), bf16),
    normed_in=((ROWS, D), bf16),
    keys=((KEYS, 128), bf16),
    vals=((KEYS, 128), bf16),
    asked=((TEAM, ROWS, 128), bf16),
    q_two=((ASKED, 128), bf16),
    graded=((TEAM, 128, ROWS), bf16),
    d_two=((ASKED, 128), bf16),
    probs=((KEYS, ASKED), f32),
    probs_b=((KEYS, ASKED), bf16),
    low_b=((KEYS, ASKED), bf16),
    part_keep=((TEAM, 128, ROWS), f32),
    low=((TEAM, 128, ROWS), bf16),
    low_land=((TEAM, 128, ROWS), bf16),
    exact=((128, ROWS), f32),
    spans=((TEAM, 2 * TEAM, 128), f32),
    deltas=((TEAM, 8, 128), f32),
    flat=((2, 2 * TEAM, 128), f32),
    shared=((TEAM, 128, ROWS), bf16),
    shared_land=((TEAM, 128, ROWS), bf16),
    context=((ROWS, 128), bf16),
    middle=((ROWS, D), bf16),
    normed_mid=((ROWS, D), bf16),
    upstream=((ROWS, HID), f32),
    activated=((ROWS, HID), bf16),
    grad_pre=((ROWS, HID), bf16),
    gmid=((ROWS, D), bf16),
    gmid_land=((2, 7, PART, D // 2), bf16),
    gmid_sum=((ROWS, D), bf16),
    down=((ROWS, D), bf16),
    down_land=((7, PART, D), bf16),
    layer=((ROWS, D), bf16),
    grad_middle=((ROWS, D), bf16),
    gq=((TEAM, 128, ROWS), bf16),
    gq_land=((TEAM - 1, 128, ROWS), bf16),
    gk=((RING, ROWS, 128), bf16),
    gv=((RING, ROWS, 128), bf16),
    gk_land=((RING - 1, ROWS, 128), bf16),
    gv_land=((RING - 1, ROWS, 128), bf16),
    grad_rows=((ROWS, 384), bf16),
    gin=((ROWS, D), bf16),
    gin_land=((2, 7, PART, D // 2), bf16),
    gin_sum=((ROWS, D), bf16),
)
WEIGHT_GRADS = dict(down=(16, D), up=(32, HID), out=(16, 256), qkv=(32, 384))
for _name, (_r, _w) in WEIGHT_GRADS.items():
    SCRATCH["wg_part_" + _name] = ((32 * _r, _w), bf16)
    SCRATCH["wg_sib_" + _name] = ((CHIPS, _r, _w), bf16)
    SCRATCH["wg_sum_" + _name] = ((CHIPS, _r, _w), bf16)
    SCRATCH["wg_land_" + _name] = ((CHIPS - 1, _r, _w), bf16)
LOADED = ("agg_key", "table", "pixels", "embed_w", "w_out", "agg_value", "w_down", "cot", "agg_out",
          "pos", "w_qkv", "w_up")
EARLY = 4
SEMS = 128


class Names:
    pass


def whole_kernel(*refs):
    mask_ref, ids_ref, query_ref = refs[:3]
    hbm = dict(zip(LOADED, refs[3 : 3 + len(LOADED)]))
    at = 3 + len(LOADED)
    layer_ref, gtok_ref, gqkv_ref, gout_ref, gup_ref, gdown_ref = refs[at : at + 6]
    at += 6
    b = Names()
    for name, ref in zip(SCRATCH, refs[at : at + len(SCRATCH)]):
        setattr(b, name, ref)
    load_sem, ss, rs = refs[at + len(SCRATCH) :]

    v = lax.axis_index("var")
    s = lax.axis_index("space")
    core = lax.rem(s, 2)
    chip = s // 2
    cx, cy = chip // 4, lax.rem(chip, 4)
    sib = s + 1 - 2 * core
    own = pl.ds(pl.multiple_of(v * PART, PART), PART)

    def chip_at(dx, dy):
        return lax.rem(cx + dx, 4) * 4 + lax.rem(cy + dy, 4)

    offsets = [(dx, dy) for dx in range(4) for dy in range(4)]
    around = {o: chip_at(*o) for o in offsets}

    used = [0]
    pending = []

    def fresh(n=1):
        used[0] += n
        assert used[0] <= SEMS
        return used[0] - n

    def wait(sem, ref):
        pltpu.make_async_copy(ref, ref, sem).wait()

    def send(src, dst, k, where):
        pltpu.make_async_remote_copy(
            src_ref=src, dst_ref=dst, send_sem=ss.at[k], recv_sem=rs.at[k],
            device_id=where, device_id_type=MESH,
        ).start()

    def to_core(c):
        return {"space": c}

    def same_core(o):
        return {"space": around[o] * 2 + core}

    loads = {}
    for i, name in enumerate(LOADED):
        loads[name] = pltpu.make_async_copy(hbm[name], getattr(b, name), load_sem.at[i])
        if i < EARLY:
            loads[name].start()

    def ready(*names):
        for name in names:
            loads[name].wait()

    barrier = pltpu.get_barrier_semaphore()
    for d in range(1, 8):
        pl.semaphore_signal(barrier, inc=1, device_id={"var": lax.rem(v + d, NV)}, device_id_type=MESH)
    for o in offsets[1:]:
        pl.semaphore_signal(barrier, inc=1, device_id=same_core(o), device_id_type=MESH)
    pl.semaphore_signal(barrier, inc=1, device_id=to_core(sib), device_id_type=MESH)
    for d in range(1, RING):
        pl.semaphore_signal(barrier, inc=1, device_id=to_core(around[0, d] * 2 + 1 - core), device_id_type=MESH)

    def z_scatter(src, land):
        k = fresh()
        for d in FAR_FIRST:
            there = lax.rem(v + d, NV)
            send(src.at[pl.ds(pl.multiple_of(there * PART, PART), PART)], land.at[d - 1], k,
                 {"var": there})
        pending.append((k, land))
        return lambda: wait(rs.at[k], land)

    def z_gather(ref):
        k = fresh()
        for d in FAR_FIRST:
            send(ref.at[own], ref.at[own], k, {"var": lax.rem(v + d, NV)})
        pending.append((k, ref.at[pl.ds(0, 7 * PART)]))
        return lambda: wait(rs.at[k], ref.at[pl.ds(0, 7 * PART)])

    class Halves:
        def __init__(self, src, land, out):
            self.src, self.land, self.out = src, land, out
            self.k = fresh(4)

        def columns(self, half):
            return pl.ds(half * (D // 2), D // 2)

        def start(self, half):
            for d in FAR_FIRST:
                there = lax.rem(v + d, NV)
                send(self.src.at[pl.ds(pl.multiple_of(there * PART, PART), PART), self.columns(half)],
                     self.land.at[half, d - 1], self.k + half, {"var": there})
            pending.append((self.k + half, self.land.at[half]))

        def turn(self, half, add=None):
            wait(rs.at[self.k + half], self.land.at[half])
            parts = [self.src[own, self.columns(half)]] + [self.land[half, d] for d in range(7)]
            if add is None:
                total = parts[0].astype(f32)
                for part in parts[1:]:
                    total = total + part.astype(f32)
            else:
                total = add(parts)
            self.out[own, self.columns(half)] = total.astype(bf16)
            for d in FAR_FIRST:
                send(self.out.at[own, self.columns(half)], self.out.at[own, self.columns(half)],
                     self.k + 2 + half, {"var": lax.rem(v + d, NV)})
            pending.append((self.k + 2 + half, self.land.at[half]))

        def finish(self):
            for half in range(2):
                wait(rs.at[self.k + 2 + half], self.land.at[half])

    def landed(src, land):
        total = src[own].astype(f32)
        for d in range(7):
            total = total + land[d].astype(f32)
        return total

    place = cy * 2 + core
    mates = []
    for d in range(1, RING):
        mates.append((around[0, d] * 2 + core, lax.rem(cy + d, 4) * 2 + core))
        mates.append((around[0, d] * 2 + 1 - core, lax.rem(cy + d, 4) * 2 + 1 - core))
    mates.append((sib, cy * 2 + 1 - core))
    ring = [(same_core((d, 0)), lax.rem(cx + d, 4)) for d in range(1, RING)]

    def team_gather(ref):
        k = fresh()
        for to, _ in mates:
            send(ref.at[place], ref.at[place], k, to_core(to))
        seven = ref.at[pl.ds(0, TEAM - 1)]
        pending.append((k, seven))
        return lambda: wait(rs.at[k], seven)

    def team_scatter(src, land):
        k = fresh()
        for j, (to, t) in enumerate(mates):
            send(src.at[t], land.at[j], k, to_core(to))
        seven = land.at[pl.ds(0, TEAM - 1)]
        pending.append((k, seven))
        return lambda: wait(rs.at[k], seven)

    def ring_gather(ref):
        k = fresh()
        rows = pl.ds(pl.multiple_of(cx * ROWS, ROWS), ROWS)
        for to, _ in ring:
            send(ref.at[rows], ref.at[rows], k, to)
        three = ref.at[pl.ds(0, 3 * ROWS)]
        pending.append((k, three))
        return lambda: wait(rs.at[k], three)

    def ring_scatter(src, land):
        k = fresh()
        for j, (to, t) in enumerate(ring):
            send(src.at[t], land.at[j], k, to)
        pending.append((k, land))
        return lambda: wait(rs.at[k], land)

    class Reduce:
        def __init__(self, name):
            self.part = getattr(b, "wg_part_" + name)
            self.sib = getattr(b, "wg_sib_" + name)
            self.sum = getattr(b, "wg_sum_" + name)
            self.land = getattr(b, "wg_land_" + name)
            self.r = WEIGHT_GRADS[name][0]
            self.k = fresh(2)

        def block(self, which, side):
            return pl.ds(pl.multiple_of((2 * which + side) * self.r, self.r), self.r)

        def start(self):
            for i in range(CHIPS):
                send(self.part.at[self.block(i, 1 - core)], self.sib.at[i], self.k, to_core(sib))
            pending.append((self.k, self.sib))

        def spread(self):
            wait(rs.at[self.k], self.sib)

            def add(i, carry):
                self.sum[i] = (self.part[self.block(i, core)].astype(f32)
                               + self.sib[i].astype(f32)).astype(bf16)
                return carry

            lax.fori_loop(0, CHIPS, add, 0)
            for j, o in enumerate(offsets[1:]):
                send(self.sum.at[around[o]], self.land.at[j], self.k + 1, same_core(o))
            pending.append((self.k + 1, self.land))

        def finish(self):
            wait(rs.at[self.k + 1], self.land)
            total = self.part[self.block(chip, core)].astype(f32) + self.sib[chip].astype(f32)
            for j in range(CHIPS - 1):
                total = total + self.land[j].astype(f32)
            return total

    ready("agg_key")
    row, lane = iota((128, D), 0), iota((128, D), 1)
    spots = (lane // DH == lax.rem(row, H)) & (row < 3 * H)
    spread_one = jnp.where(spots, 1.0, 0.0).astype(bf16)
    rest = jnp.where(spots, query_ref[...], 0.0)
    dirs = jnp.zeros((32, 128), f32)
    for _ in range(3):
        piece = rest.astype(bf16)
        dirs = dirs + nt(b.agg_key[...], piece)
        rest = rest - piece.astype(f32)
    b.dirs_part[...] = dirs.astype(bf16)
    b.dirs_land[0, 0] = dirs.astype(bf16)

    ready("table")
    row, lane = iota((16, V), 0), iota((16, V), 1)
    picks = jnp.zeros((16, V), f32)
    for i in range(SLOTS):
        picks = picks + jnp.where((row == i) & (lane == ids_ref[i]), 1.0, 0.0)
    b.table_rows[...] = nn(picks.astype(bf16), b.table[...])
    ready("pixels", "embed_w")
    for name in LOADED[EARLY:]:
        loads[name].start()

    def embed(i, carry):
        raw = tn(b.pixels[i], b.embed_w[i])
        b.embedded[pl.ds(pl.multiple_of(i * ROWS, ROWS), ROWS)] = (
            raw + b.table_rows[pl.ds(i, 1)]).astype(bf16)
        return carry

    lax.fori_loop(0, SLOTS, embed, 0, unroll=3)
    pl.semaphore_wait(barrier, 7 + CHIPS - 1 + 1 + RING - 1)
    dirs_k = fresh(2)
    for j, o in enumerate(offsets[1:]):
        send(b.dirs_part, b.dirs_land.at[0, j + 1], dirs_k, same_core(o))
    pending.append((dirs_k, b.dirs_land.at[0, pl.ds(1, CHIPS - 1)]))

    ready("w_out")
    columns = pl.ds(pl.multiple_of(cx * 256, 256), 256)
    piece = pl.ds(pl.multiple_of(place * PART, PART), PART)
    full_k = fresh(CHIPS + 1)
    for d in FAR_FIRST:
        send(b.w_out.at[piece, columns], b.w_full.at[v, cy, core, :, columns], full_k,
             {"var": lax.rem(v + d, NV)})
    b.w_full[v, cy, core, :, columns] = b.w_out[piece, columns]
    seven = b.w_full.at[pl.ds(0, NV - 1), 0, 0, :, pl.ds(0, 256)]
    eight = b.w_full.at[:, 0, 0, :, pl.ds(0, 256)]
    pending.append((full_k, seven))


    ready("agg_value")

    def value_columns(i, carry):
        columns = pl.ds(pl.multiple_of(i * 256, 256), 256)
        for m in range(2):
            these = pl.ds(m * 768, 768)
            b.values[these, columns] = nn(b.embedded[these], b.agg_value[:, columns])
        return carry

    lax.fori_loop(0, 3, value_columns, 0)
    wait(rs.at[dirs_k], b.dirs_land.at[0, pl.ds(1, CHIPS - 1)])
    send(b.dirs_land.at[0], b.dirs_land.at[1], dirs_k + 1, to_core(sib))
    pending.append((dirs_k + 1, b.dirs_land.at[1]))
    wait(rs.at[full_k], seven)
    for j, o in enumerate(offsets[1:]):
        send(b.w_full.at[:, cy, core, :, columns], b.w_full.at[:, cy, core, :, columns],
             full_k + 1 + j, same_core(o))
        pending.append((full_k + 1 + j, eight))
    value_columns(3, 0)
    wait(rs.at[dirs_k + 1], b.dirs_land.at[1])
    for j, o in enumerate(offsets):
        source = lax.rem(cx - o[0] + 4, 4) * 4 + lax.rem(cy - o[1] + 4, 4)
        for side in range(2):
            owner = 2 * source + (core if side == 0 else 1 - core)
            b.dirs[pl.ds(pl.multiple_of(owner * 32, 32), 32)] = b.dirs_land[side, j]

    b.scores[...] = nn(b.embedded[...], b.dirs[...]) * DH ** (-0.5)
    lane = iota((ROWS, 128), 1)
    top = jnp.full((ROWS, 128), MASK_FLOOR, f32)
    for i in range(SLOTS):
        rows = pl.ds(i * ROWS, ROWS)
        top = jnp.maximum(top, jnp.where(mask_ref[i] > 0, b.scores[rows], MASK_FLOOR))
    total = jnp.zeros((ROWS, 128), f32)
    for i in range(SLOTS):
        rows = pl.ds(i * ROWS, ROWS)
        weight = jnp.where(mask_ref[i] > 0, jnp.exp(
            jnp.where(mask_ref[i] > 0, b.scores[rows], MASK_FLOOR) - top), 0.0)
        b.scores[rows] = weight
        total = total + weight
    scale = 1.0 / total
    b.level[...] = top + jnp.log(total)
    for i in range(SLOTS):
        rows = pl.ds(i * ROWS, ROWS)
        b.shares[rows] = thirds(b.scores[rows] * scale, lane)
    level_in = z_scatter(b.level, b.level_land)
    pooled = Halves(b.pooled, b.pooled_land, b.mixed)
    for c in range(4):
        columns = slice(c * 256, (c + 1) * 256)
        wide = nn(b.shares[...], spread_one[:, columns])
        acc = jnp.zeros((ROWS, 256), f32)
        for i in range(SLOTS):
            acc = acc + wide[i * ROWS : (i + 1) * ROWS] * b.values[pl.ds(i * ROWS, ROWS), columns]
        b.pooled[:, columns] = acc.astype(bf16)
        if c % 2:
            pooled.start(c // 2)

    ready("w_down", "cot")
    b.upstream[...] = nt(b.cot[...], b.w_down[...])
    ready("agg_out", "pos")
    level_in()
    levels = [b.level[own]] + [b.level_land[d] for d in range(7)]
    top = functools.reduce(jnp.maximum, levels)
    lifts = [jnp.exp(x - top) for x in levels]
    scale = 1.0 / sum(lifts[1:], lifts[0])
    lane = iota((PART, 128), 1)
    lifts = [nn(thirds(x * scale, lane), spread_one) for x in lifts]
    half = D // 2
    for h in range(2):
        pooled.turn(h, lambda parts: sum(
            lifts[i][:, h * half : (h + 1) * half] * parts[i].astype(f32) for i in range(NV)))
    for j in range(CHIPS - 1):
        wait(rs.at[full_k + 1 + j], eight)
    send(b.w_full.at[:, :, core], b.w_full.at[:, :, core], full_k + CHIPS, to_core(sib))
    pending.append((full_k + CHIPS, b.w_full.at[:, :, 0]))
    ready("w_qkv", "w_up")
    pooled.finish()
    b.tokens[...] = (nn(b.mixed[...], b.agg_out[...]) + b.pos[...].astype(f32)).astype(bf16)

    b.normed_in[...] = layer_norm(b.tokens[...]).astype(bf16)
    mine = pl.ds(pl.multiple_of(cx * ROWS, ROWS), ROWS)
    b.asked[place] = nn(b.normed_in[...], b.w_qkv[0]).astype(bf16) * DH ** (-0.5)
    asked_in = team_gather(b.asked)
    b.keys[mine] = nn(b.normed_in[...], b.w_qkv[1]).astype(bf16)
    keys_in = ring_gather(b.keys)
    b.vals[mine] = nn(b.normed_in[...], b.w_qkv[2]).astype(bf16)
    vals_in = ring_gather(b.vals)

    def chunk(i):
        return pl.ds(pl.multiple_of(i * CHUNK, CHUNK), CHUNK)

    def eights(x):
        return x.reshape(CHUNK // 8, 8, ASKED)

    def stretch(ref, t):
        return jnp.concatenate([ref[t, pl.ds(r, 1), :] for r in range(2 * TEAM)], 1)

    lane = iota((ROWS, 128), 1)
    zero = jnp.zeros((ROWS, 128), bf16)

    def two(ref, block):
        for t in range(TEAM):
            ref[pl.ds(t * ROWS, ROWS)] = jnp.where(lane < DH, block(t), zero)
            ref[pl.ds((TEAM + t) * ROWS, ROWS)] = jnp.where(lane < DH, zero, block(t))

    asked_in()
    two(b.q_two, lambda t: b.asked[t])
    keys_in()
    steps = KEYS // CHUNK

    def score_step(i, top):
        part = nt(b.keys[chunk(i)], b.q_two[...])
        b.probs[chunk(i)] = part
        return jnp.maximum(top, jnp.max(eights(part), 0))

    top = lax.fori_loop(0, steps, score_step, jnp.full((8, ASKED), -jnp.inf, f32))
    top = jnp.max(top, 0, keepdims=True)

    def exp_step(i, total):
        part = jnp.exp(b.probs[chunk(i)] - top)
        b.probs[chunk(i)] = part
        b.probs_b[chunk(i)] = part.astype(bf16)
        return total + jnp.sum(eights(part), 0)

    total = lax.fori_loop(0, steps, exp_step, jnp.zeros((8, ASKED), f32))
    total = jnp.sum(total, 0, keepdims=True)
    span = top + jnp.log(total)
    for r in range(2 * TEAM):
        b.spans[place, pl.ds(r, 1), :] = span[:, r * 128 : (r + 1) * 128]
    spans_in = team_gather(b.spans)
    vals_in()
    scale = 1.0 / total
    for h in range(2):
        side = slice(h * TEAM * ROWS, (h + 1) * TEAM * ROWS)
        part = tn(b.vals[...], b.probs_b[:, side]) * scale[:, side]
        for t in range(TEAM):
            here = part[h * DH : (h + 1) * DH, t * ROWS : (t + 1) * ROWS]
            b.part_keep[t, h * DH : (h + 1) * DH, :] = here
            b.shared[t, h * DH : (h + 1) * DH, :] = here.astype(bf16)
    shared_in = team_scatter(b.shared, b.shared_land)

    def low_step(i, carry):
        b.low_b[chunk(i)] = (b.probs[chunk(i)] - b.probs_b[chunk(i)].astype(f32)).astype(bf16)
        return carry

    lax.fori_loop(0, steps, low_step, 0)
    for h in range(2):
        side = slice(h * TEAM * ROWS, (h + 1) * TEAM * ROWS)
        part = tn(b.vals[...], b.low_b[:, side]) * scale[:, side]
        rows = slice(h * DH, (h + 1) * DH)
        for t in range(TEAM):
            b.low[t, rows, :] = (part[rows, t * ROWS : (t + 1) * ROWS] + (
                b.part_keep[t, rows, :] - b.shared[t, rows, :].astype(f32))).astype(bf16)
    low_in = team_scatter(b.low, b.low_land)
    spans_in()
    all_spans = b.spans[...]
    top = jnp.max(all_spans, 0)
    whole_span = top + jnp.log(jnp.sum(jnp.exp(all_spans - top[None]), 0))
    shared_in()

    def lift(t):
        rows = [pl.ds(h * TEAM + place, 1) for h in range(2)]
        each = [jnp.exp(b.spans[t, rows[h], :] - b.flat[0, rows[h], :]) for h in range(2)]
        return jnp.where(iota((128, ROWS), 0) < DH, each[0], each[1])

    b.flat[0] = whole_span
    lifted = [lift(place)]
    acc = lifted[0] * b.shared[place].astype(f32)
    for j, (_, t) in enumerate(mates):
        back = lax.rem(cy + 4 - (j // 2 + 1), 4) * 2 + (core if j % 2 == 0 else 1 - core)
        lifted.append(lift(back if j < 6 else t))
        acc = acc + lifted[-1] * b.shared_land[j].astype(f32)
    b.context[...] = acc.T.astype(bf16)
    b.context_all[v] = b.context[...]

    k = fresh()
    seven = b.context_all.at[pl.ds(0, NV - 1)]
    for d in FAR_FIRST:
        send(b.context_all.at[v], b.context_all.at[v], k, {"var": lax.rem(v + d, NV)})
    pending.append((k, seven))
    factor = jnp.exp(span - stretch(b.flat, 0)) * scale

    def norm_step(i, carry):
        part = b.probs[chunk(i)] * factor
        b.probs[chunk(i)] = part
        b.probs_b[chunk(i)] = part.astype(bf16)
        return carry

    lax.fori_loop(0, steps, norm_step, 0)
    low_in()
    acc = acc + lifted[0] * b.low[place].astype(f32)
    for j in range(TEAM - 1):
        acc = acc + lifted[j + 1] * b.low_land[j].astype(f32)
    b.exact[...] = acc
    wait(rs.at[full_k + CHIPS], b.w_full.at[:, :, 0])
    wait(rs.at[k], seven)
    all_context = jnp.concatenate([b.context_all[i] for i in range(NV)], 1)
    b.middle[...] = (b.tokens[...].astype(f32)
                     + nn(all_context, b.w_full[...].reshape(D, D))).astype(bf16)

    b.normed_mid[...] = layer_norm(b.middle[...]).astype(bf16)
    pre = nn(b.normed_mid[...], b.w_up[...])
    half = 0.5 * (1.0 + lax.erf(pre * 0.5 ** 0.5))
    b.activated[...] = (pre * half).astype(bf16)
    slope = half + pre * (jnp.exp(-0.5 * pre * pre) * 0.3989422804014327)
    b.grad_pre[...] = (b.upstream[...] * slope).astype(bf16)
    gmid = Halves(b.gmid, b.gmid_land, b.gmid_sum)
    for h in range(2):
        half = pl.ds(h * (D // 2), D // 2)
        b.gmid[:, half] = nt(b.grad_pre[...], b.w_up[half]).astype(bf16)
        gmid.start(h)
    b.down[...] = nn(b.activated[...], b.w_down[...]).astype(bf16)
    wg = {name: Reduce(name) for name in WEIGHT_GRADS}
    wg["down"].part[...] = tn(b.activated[...], b.cot[...]).astype(bf16)
    wg["down"].start()
    gmid.turn(0)
    gmid.turn(1)
    wg["up"].part[...] = tn(b.normed_mid[...], b.grad_pre[...]).astype(bf16)
    wg["up"].start()
    wg["down"].spread()
    gmid.finish()
    b.grad_middle[...] = (b.cot[...].astype(f32) + norm_back(
        b.middle[...], b.gmid_sum[...].astype(f32))).astype(bf16)

    b.graded[place] = nt(b.grad_middle[...], b.w_out[...]).astype(bf16)
    graded_in = team_gather(b.graded)
    products = b.graded[place].astype(f32).T * b.exact[...]
    b.deltas[place] = jnp.zeros((8, 128), f32)
    for h in range(2):
        b.deltas[place, pl.ds(h, 1), :] = jnp.sum(products[h * DH : (h + 1) * DH], 0, keepdims=True)
    deltas_in = team_gather(b.deltas)
    down_in = z_scatter(b.down, b.down_land)
    row, lane5 = iota((128, 512), 0), iota((128, 512), 1)
    total = jnp.zeros((512, 256), f32)
    for q in range(4):
        pick = (lane5 // 16 == row // 4) & (lax.rem(lane5, 16) == q * 4 + lax.rem(row, 4))
        picked = nn(b.context[...], jnp.where(pick, 1.0, 0.0).astype(bf16)).astype(bf16)
        total = total + tn(picked, b.grad_middle[:, q * 256 : (q + 1) * 256])
    wg["out"].part[...] = total.astype(bf16)
    wg["out"].start()
    graded_in()
    two(b.d_two, lambda t: b.graded[t])

    for t in range(RING):
        b.gv[t] = nn(b.probs_b[pl.ds(t * ROWS, ROWS)], b.d_two[...]).astype(bf16)
    gv_in = ring_scatter(b.gv, b.gv_land)
    deltas_in()
    delta = jnp.concatenate(
        [b.deltas[t, pl.ds(h, 1), :] for h in range(2) for t in range(TEAM)], 1)

    def back_step(i, carry):
        part = nt(b.vals[chunk(i)], b.d_two[...])
        b.probs_b[chunk(i)] = (b.probs[chunk(i)] * (part - delta)).astype(bf16)
        return carry

    lax.fori_loop(0, steps, back_step, 0)
    for h in range(2):
        side = slice(h * TEAM * ROWS, (h + 1) * TEAM * ROWS)
        part = tn(b.keys[...], b.probs_b[:, side])
        for t in range(TEAM):
            b.gq[t, h * DH : (h + 1) * DH, :] = (
                part[h * DH : (h + 1) * DH, t * ROWS : (t + 1) * ROWS].astype(bf16))
    gq_in = team_scatter(b.gq, b.gq_land)
    for t in range(RING):
        b.gk[t] = nn(b.probs_b[pl.ds(t * ROWS, ROWS)], b.q_two[...]).astype(bf16)
    gk_in = ring_scatter(b.gk, b.gk_land)

    down_in()
    b.layer[own] = (b.middle[own].astype(f32) + landed(b.down, b.down_land)).astype(bf16)
    layer_in = z_gather(b.layer)
    wg["up"].spread()
    wg["out"].spread()
    for c, part, land, come in ((2, b.gv, b.gv_land, gv_in), (0, b.gq, b.gq_land, gq_in), (1, b.gk, b.gk_land, gk_in)):
        come()
        total = part[cx if c else place].astype(f32)
        for j in range(RING - 1 if c else TEAM - 1):
            total = total + land[j].astype(f32)
        if c == 0:
            total = total.T * DH ** (-0.5)
        b.grad_rows[:, c * 128 : (c + 1) * 128] = total.astype(bf16)

    gin = Halves(b.gin, b.gin_land, b.gin_sum)
    for h in range(2):
        half = pl.ds(h * (D // 2), D // 2)
        b.gin[:, half] = sum(
            nt(b.grad_rows[:, c * 128 : (c + 1) * 128], b.w_qkv[c, half]) for c in (1, 2, 0)).astype(bf16)
        gin.start(h)
    wg["qkv"].part[...] = tn(b.normed_in[...], b.grad_rows[...]).astype(bf16)
    wg["qkv"].start()
    gdown_ref[...] = wg["down"].finish()
    wg["qkv"].spread()
    gin.turn(0)
    gin.turn(1)
    layer_in()
    layer_ref[...] = b.layer[...]
    gup_ref[...] = wg["up"].finish()
    total = wg["out"].finish()
    for q in range(4):
        gout_ref[:, q * 256 : (q + 1) * 256] = total[q * 4 : (q + 1) * 4]
    total = wg["qkv"].finish()
    for c in range(3):
        gqkv_ref[c] = total[:, c * 128 : (c + 1) * 128]
    for k, ref in pending:
        wait(ss.at[k], ref)
    gin.finish()
    gtok_ref[...] = (b.grad_middle[...].astype(f32) + norm_back(
        b.tokens[...], b.gin_sum[...].astype(f32))).astype(bf16)


def hand_over(*refs):
    for i in range(6):
        refs[6 + i][...] = refs[i][...]


def shards(pixels, valid_mask, var_ids, embed_weight, var_table, agg_query, agg_key,
           agg_value, agg_out, pos_embed, w_qkv, w_out, w_up, w_down, cotangent):
    in_vmem = pl.BlockSpec(memory_space=pltpu.VMEM)
    in_smem = pl.BlockSpec(memory_space=pltpu.SMEM)
    anywhere = pl.BlockSpec(memory_space=pl.ANY)
    big = (agg_key, var_table, pixels, embed_weight, w_out, agg_value, w_down, cotangent, agg_out,
           pos_embed, w_qkv.transpose(1, 0, 2), w_up)
    shape = jax.ShapeDtypeStruct
    outs = pl.pallas_call(
        whole_kernel,
        out_shape=[shape((ROWS, D), bf16), shape((ROWS, D), bf16), shape((3, 32, 128), f32),
                   shape((4, D), f32), shape((32, HID), f32), shape((16, D), f32)],
        in_specs=[in_smem, in_smem, in_vmem] + [anywhere] * len(big),
        out_specs=[in_vmem] * 6,
        scratch_shapes=[pltpu.VMEM(*spec) for spec in SCRATCH.values()]
        + [pltpu.SemaphoreType.DMA((len(LOADED),)), pltpu.SemaphoreType.DMA((SEMS,)),
           pltpu.SemaphoreType.DMA((SEMS,))],
        compiler_params=pltpu.CompilerParams(
            collective_id=0, has_side_effects=True, vmem_limit_bytes=60 * 2**20),
        name="whole",
    )(valid_mask, var_ids, agg_query.reshape(1, D), *big)
    layer_out, grad_tokens, grad_qkv, grad_out, grad_up, grad_down = pl.pallas_call(
        hand_over,
        out_shape=[shape(x.shape, x.dtype) for x in outs],
        in_specs=[in_vmem] * 6,
        out_specs=[in_vmem] * 6,
        name="hand_over",
    )(*outs)
    return (layer_out, grad_tokens, grad_qkv.transpose(1, 0, 2), grad_out, grad_up, grad_down)


def solution(mesh):
    in_specs = (
        P("var", None, "space"), P("var"), P("var"), P("var", None, None), P(), P(),
        P("space", None), P(), P(), P("space", None), P(None, None, "var"), P("var", None),
        P(None, "var"), P("var", None), P("space", None),
    )
    out_specs = (
        P("space", None), P("space", None), P("space", None, "var"),
        P(("var", "space"), None), P("space", "var"), P(("var", "space"), None),
    )
    return jax.shard_map(shards, mesh=mesh, in_specs=in_specs, out_specs=out_specs, check_vma=False)
```
